512 devices in a mesh: inst: 64 (over x, z), tp: 8 (over y, core).
Axes of the slice: x: 4, y: 4, z: 16, core: 2. Of those that a mesh axis runs over, the one named last changes fastest.
Arguments:
- kv_cache: bfloat16 [1024, 64, 2048], P('inst', 'tp'), may hold values from -6 to 6
- route: int32 [1024], P('inst'), may hold values from 0 to 63, as said below
- queries: bfloat16 [4096, 6144], P('inst', 'tp'), may hold values from -110 to 110
- fresh_kv: bfloat16 [4096, 2048], P('inst', 'tp'), may hold values from -6 to 6
- picked: int32 [2048, 2], P('inst'), may hold values from 0 to 63, as said below
Outputs:
- attn_out: bfloat16 [4096, 6144], P('inst', 'tp')
- updated_cache: bfloat16 [1024, 64, 2048], P('inst', 'tp')
The draws below stay inside these ranges and needn't reach their ends.
Inputs may be any that keep to these rules, and one draw needn't show every extreme that they name: `route`: one holder's 16 blocks go at most 2 to one executor, and some holder sends exactly 2 to some executor. One executor receives at most 32 blocks in all, and some executor exactly 32; every executor receives at least one. `picked`: the 2 positions of one row are distinct.
All inputs are finite; a program needn't handle non-finite values.
Results may differ from the reference program's by a relative error of at most 0.013.
Values may be sent and summed in bfloat16 or wider, within the bound.
No kernel may reach another device: no remote copies, remote signals or barrier semaphores. Data moves between devices by JAX's collectives and lax.ppermute only.
A program may use at most 64 MiB of HBM per device.

```python
import math
import jax
import jax.numpy as jnp
from jax import lax

KVH = 8
HD = 128
QH = 6
BLK = 64
HOLD = 16
SELB = 2
SLOT = 2
MAXREC = 32
ROWS = 64
BLOCKS = 1024
N_INST = 64


def draw_route(key, part):
    key = jax.random.fold_in(key, 11)
    key_order, key_shuffle = jax.random.split(key)
    quarter = N_INST // 4
    pattern = jnp.concatenate([jnp.full((quarter,), 2 * HOLD, jnp.int32), jnp.full((quarter,), HOLD // 2, jnp.int32), jnp.full((N_INST - 2 * quarter,), 3 * HOLD // 4, jnp.int32)])
    order = jax.random.permutation(key_order, N_INST).astype(jnp.int32)
    owners = jnp.repeat(order, pattern, total_repeat_length=N_INST * HOLD)
    tokens = jnp.arange(N_INST * HOLD, dtype=jnp.int32)
    holder = tokens // SLOT % N_INST
    place = tokens // (SLOT * N_INST) * SLOT + tokens % SLOT
    table = jnp.zeros((N_INST, HOLD), jnp.int32).at[holder, place].set(owners)
    shuffles = jax.vmap(lambda subkey: jax.random.permutation(subkey, HOLD))(jax.random.split(key_shuffle, N_INST))
    table = jnp.take_along_axis(table, shuffles.astype(jnp.int32), axis=1)
    return table.reshape(N_INST * HOLD).astype(jnp.int32)


def draw_picked(key, part):
    key = jax.random.fold_in(key, 12)
    subkeys = jax.random.split(key, N_INST * MAXREC)
    chosen = jax.vmap(lambda subkey: jax.random.permutation(subkey, BLK)[:SELB])(subkeys)
    return chosen.astype(jnp.int32)


def draw_queries(key, part):
    key = jax.random.fold_in(key, 13)
    key_values = jax.random.fold_in(key, 0)
    shape = (N_INST * ROWS, KVH * QH * HD)
    values = jnp.clip(jax.random.normal(key_values, shape, jnp.float32), -6.0, 6.0)
    return values.astype(jnp.bfloat16)


def levels(own_key, shape, cuts, least, top_value):
    level, own = 1.0, jax.random.fold_in(own_key, 6)
    for dim, blocks in cuts:
        draws = jnp.exp(jax.random.uniform(jax.random.fold_in(own, dim), (blocks,), jnp.float32, least / len(cuts), top_value / len(cuts)))
        level = level * jnp.repeat(draws, shape[dim] // blocks).reshape([-1 if axis == dim else 1 for axis in range(len(shape))])
    return level


def bell_draw(key, extent, deviation, most, cuts=(), kind=jnp.bfloat16):
    factor_of = levels(key, extent, cuts, -0.22, 0.18) if cuts else 1.0
    result = jax.random.normal(key, extent, jnp.float32) * deviation * factor_of
    return jnp.minimum(jnp.maximum(result, -most), most).astype(kind)


def setup_inputs(seed: int = 0) -> dict:
    seeds = jax.random.split(jax.random.key(seed), 6)
    return {
        "kv_cache": bell_draw(seeds[0], (BLOCKS, BLK, KVH * 2 * HD), 1.0, 6.0, ((0, 64), (1, 8))),
        "route": draw_route(jax.random.fold_in(seeds[5], 71), 0),
        "queries": draw_queries(jax.random.fold_in(seeds[5], 71), 0),
        "fresh_kv": bell_draw(seeds[3], (N_INST * ROWS, KVH * 2 * HD), 1.0, 6.0, ((0, 64), (1, 8))),
        "picked": draw_picked(jax.random.fold_in(seeds[5], 71), 0),
    }


THETA = 1000000.0

def rotate_pairs(values, shift):
    half = values.shape[-1] // 2
    freqs = jnp.power(jnp.float32(THETA), -2.0 * jnp.arange(half, dtype=jnp.float32) / values.shape[-1])
    angle = shift * freqs
    cosine = jnp.cos(angle)
    sine = jnp.sin(angle)
    first = values[..., :half]
    second = values[..., half:]
    return jnp.concatenate([first * cosine - second * sine, second * cosine + first * sine], axis=-1)

def ranks_within(table):
    equal = table[..., :, None] == table[..., None, :]
    index = jnp.arange(table.shape[-1], dtype=jnp.int32)
    earlier = index[:, None] > index[None, :]
    return lax.optimization_barrier(jnp.sum((equal & earlier).astype(jnp.int32), axis=-1)).astype(jnp.int32)

def context_slots(table, owner, maxrec):
    matched = table == owner
    counts = lax.optimization_barrier(jnp.sum(matched.astype(jnp.int32), axis=1)).astype(jnp.int32)
    inclusive = jnp.cumsum(counts).astype(jnp.int32)
    starts = inclusive - counts
    total = inclusive[-1]
    position = jnp.arange(maxrec, dtype=jnp.int32)
    holder_of = lax.optimization_barrier(jnp.sum((inclusive[None, :] <= position[:, None]).astype(jnp.int32), axis=1)).astype(jnp.int32)
    holder_of = jnp.minimum(holder_of, table.shape[0] - 1)
    slot_of = position - starts[holder_of]
    live = position < total
    return (holder_of, slot_of, live, matched, total)

def blend_context(context, fresh_rows, chosen, block_len):
    maxrec = context.shape[0]
    shift = (jnp.arange(maxrec, dtype=jnp.float32) * block_len).reshape(maxrec, 1, 1, 1)
    keys = rotate_pairs(context[:, :, :, 0, :].astype(jnp.float32), shift).astype(jnp.bfloat16)
    merged = jnp.stack([keys, context[:, :, :, 1, :]], axis=3)
    index = jnp.arange(maxrec, dtype=jnp.int32)[:, None]
    return merged.at[index, chosen].set(fresh_rows)

def return_rows(fresh_rows, block_len):
    maxrec = fresh_rows.shape[0]
    shift = (jnp.arange(maxrec, dtype=jnp.float32) * block_len).reshape(maxrec, 1, 1, 1)
    keys = rotate_pairs(fresh_rows[:, :, :, 0, :].astype(jnp.float32), -shift).astype(jnp.bfloat16)
    merged = jnp.stack([keys, fresh_rows[:, :, :, 1, :]], axis=3)
    return merged.reshape(maxrec, fresh_rows.shape[1], -1)

def attend_heads(query_heads, key_heads, value_heads, group, allowed):
    scale = 1.0 / math.sqrt(query_heads.shape[-1])

    def one_head(head_idx):
        query_rows = query_heads[head_idx]
        key_rows = key_heads[head_idx // group]
        value_rows = value_heads[head_idx // group]
        scores = lax.dot_general(query_rows, key_rows, (((1,), (1,)), ((), ())), preferred_element_type=jnp.float32) * scale
        scores = jnp.where(allowed, scores, -1e+30)
        peak = lax.optimization_barrier(jnp.max(scores, axis=1, keepdims=True))
        weights = jnp.exp(scores - peak)
        total = lax.optimization_barrier(jnp.sum(weights, axis=1, keepdims=True))
        mixed = jnp.dot(weights.astype(jnp.bfloat16), value_rows, preferred_element_type=jnp.float32)
        return mixed / total
    return lax.map(one_head, jnp.arange(query_heads.shape[0], dtype=jnp.int32))

def attention_block(merged, queries_dev, chosen, live, total, block_len, group):
    maxrec = merged.shape[0]
    heads_kv = merged.shape[2]
    head_size = merged.shape[4]
    rows = queries_dev.shape[0]
    key_heads = merged[:, :, :, 0, :].reshape(maxrec * block_len, heads_kv, head_size).transpose(1, 0, 2)
    value_heads = merged[:, :, :, 1, :].reshape(maxrec * block_len, heads_kv, head_size).transpose(1, 0, 2)
    query_heads = queries_dev.reshape(rows, heads_kv * group, head_size).transpose(1, 0, 2)
    key_pos = jnp.arange(maxrec * block_len, dtype=jnp.int32)
    key_live = key_pos < total * block_len
    query_pos = (jnp.arange(maxrec, dtype=jnp.int32)[:, None] * block_len + chosen).reshape(rows)
    allowed = key_live[None, :] & (key_pos[None, :] <= query_pos[:, None])
    mixed = attend_heads(query_heads, key_heads, value_heads, group, allowed)
    mixed = mixed.transpose(1, 0, 2).reshape(rows, heads_kv * group * head_size)
    row_live = jnp.repeat(live, chosen.shape[1])
    return jnp.where(row_live[:, None], mixed, 0.0).astype(jnp.bfloat16)

def reference(kv_cache, route, queries, fresh_kv, picked):
    table = route.reshape(N_INST, HOLD)
    ranks = ranks_within(table)
    local_index = jnp.arange(HOLD, dtype=jnp.int32)

    def per_executor(owner):
        holder_of, slot_of, live, matched, total = context_slots(table, owner, MAXREC)
        choose = matched[holder_of] & (ranks[holder_of] == slot_of[:, None])
        local = lax.optimization_barrier(jnp.sum(jnp.where(choose, local_index[None, :], 0), axis=1)).astype(jnp.int32)
        block_ids = (holder_of * HOLD + local).astype(jnp.int32)
        context = kv_cache[block_ids].reshape(MAXREC, BLK, KVH, 2, HD)
        fresh_rows = lax.dynamic_slice_in_dim(fresh_kv, owner * ROWS, ROWS, 0).reshape(MAXREC, SELB, KVH, 2, HD)
        chosen = lax.dynamic_slice_in_dim(picked, owner * MAXREC, MAXREC, 0)
        queries_dev = lax.dynamic_slice_in_dim(queries, owner * ROWS, ROWS, 0)
        merged = blend_context(context, fresh_rows, chosen, BLK)
        output = attention_block(merged, queries_dev, chosen, live, total, BLK, QH)
        back = return_rows(fresh_rows, BLK)
        target = jnp.where(live, block_ids, BLOCKS).astype(jnp.int32)
        return (output, target, back)
    outputs, targets, backs = lax.map(per_executor, jnp.arange(N_INST, dtype=jnp.int32))
    attn_out = outputs.reshape(N_INST * ROWS, KVH * QH * HD)
    positions = picked.reshape(N_INST, MAXREC, SELB)
    target_rows = jnp.broadcast_to(targets[:, :, None], positions.shape)
    updated_cache = kv_cache.at[target_rows, positions].set(backs, mode='drop')
    return (attn_out, updated_cache)
```

```python
import functools
import math

import jax
import jax.numpy as jnp
from jax import lax
from jax.experimental import pallas as pl
from jax.experimental.pallas import tpu as pltpu
from jax.sharding import PartitionSpec as P

HD = 128
QH = 6
THETA = 1000000.0
CTX = 32
UNITS = 36
VMEM = pl.BlockSpec(memory_space=pltpu.VMEM)
SMEM = pl.BlockSpec(memory_space=pltpu.SMEM)
PARAMS = pltpu.CompilerParams(vmem_limit_bytes=40 * 1024 * 1024)


def spread_kernel(own_ref, x_ref, ctrl_ref, out_ref):
    y = own_ref[1]

    def step(g, carry):
        for k in range(2):
            block = lax.rem(g - y + 8, 8) + 8 * k
            for head in range(8):
                for kv in range(2):
                    lane = head * 256 + kv * 128
                    for pair in range(4):
                        dest = (kv * 32 + g * 4 + pair) * 8 + head
                        out_ref[dest, k] = x_ref[
                            block, pl.ds(2 * pair, 2), pl.ds(lane, 128)
                        ]
        return carry

    lax.fori_loop(0, 8, step, 0)
    ctrl = ctrl_ref[...]

    def fill(d, carry):
        out_ref[d, 2] = ctrl
        return carry

    lax.fori_loop(0, 512, fill, 0, unroll=16)


def tables_kernel(own_ref, ctrl_ref, tab_ref, slot_ref):
    own = own_ref[0].astype(jnp.float32)
    ctrl = ctrl_ref[...].astype(jnp.float32)
    lane = lax.broadcasted_iota(jnp.int32, (64, 128), 1)
    lanef = lane.astype(jnp.float32)
    routes = [ctrl[:, l : l + 1] for l in range(16)]
    masks = [jnp.where(r == lanef, 1.0, 0.0) for r in routes]
    counts = functools.reduce(lambda a, b: a + b, masks)
    row = lax.broadcasted_iota(jnp.int32, (64, 64), 0)
    col = lax.broadcasted_iota(jnp.int32, (64, 64), 1)
    lower = jnp.where(col < row, 1.0, 0.0).astype(jnp.bfloat16)
    starts = jnp.dot(
        lower, counts.astype(jnp.bfloat16), preferred_element_type=jnp.float32
    )
    tab = jnp.zeros((64, 128), jnp.float32)
    slots = jnp.zeros((64, 128), jnp.float32)
    seen = jnp.zeros((64, 128), jnp.float32)
    for l in range(16):
        within = jnp.sum(masks[l] * seen, axis=1, keepdims=True)
        rank = jnp.sum(masks[l] * starts, axis=1, keepdims=True) + within
        seen = seen + masks[l]
        tab = jnp.where(lane == l, routes[l] * UNITS + rank, tab)
        tab = jnp.where(lane == 32 + l, within, tab)
        tab = jnp.where(lane == 48 + l, rank, tab)
        mine = (routes[l] == own) & (rank == lanef)
        slots = slots + jnp.where(mine, float(l), 0.0)
    own_lane = lanef == own
    first = jnp.sum(jnp.where(own_lane, starts, 0.0), axis=1, keepdims=True)
    tab = jnp.where(lane == 16, first, tab)
    tab_ref[...] = tab.astype(jnp.int32)
    locals_ = jnp.sum(slots, axis=0, keepdims=True)
    total = jnp.sum(jnp.where(own_lane, counts, 0.0))
    row8 = lax.broadcasted_iota(jnp.int32, (8, 128), 0)
    slot_ref[...] = jnp.where(row8 == 0, locals_, total).astype(jnp.int32)


def dispatch_kernel(own_ref, tab_ref, r_ref, back_ref, out_ref):
    g = lax.rem(own_ref[0] // 4, 8)

    def step(h, carry):
        for y in range(8):
            block = lax.rem(g - y + 8, 8)
            for k in range(2):
                out_ref[tab_ref[h, block + 8 * k]] = r_ref[h * 8 + y, k]
        first = tab_ref[h, 16]
        for s in range(2):
            slot = jnp.minimum(first + s, CTX - 1)
            for kv in range(2):
                out_ref[h * UNITS + CTX + 2 * s + kv] = back_ref[slot, kv]
        return carry

    lax.fori_loop(0, 64, step, 0)


def attention_kernel(
    total_ref, recv_ref, q_ref, f0_ref, f1_ref, i0_ref, i1_ref,
    cos_ref, sin_ref, kpos_ref, qpos_ref, out_ref, keys, vals,
):
    total = total_ref[0]
    cos = cos_ref[...]
    sin = sin_ref[...]
    pick0 = i0_ref[...]
    pick1 = i1_ref[...]
    live = lax.broadcasted_iota(jnp.int32, (64, 128), 0) < 2 * total
    k0 = f0_ref[:, :128].astype(jnp.float32)
    k1 = f1_ref[:, :128].astype(jnp.float32)
    v0 = f0_ref[:, 128:].astype(jnp.float32)
    v1 = f1_ref[:, 128:].astype(jnp.float32)
    for i in range(32):
        at0 = pick0 == i
        at1 = pick1 == i
        k = recv_ref[i, :CTX].reshape(64, 128).astype(jnp.float32)
        k = k * cos + pltpu.roll(k, 64, 1) * sin
        k = jnp.where(at0, k0, jnp.where(at1, k1, k))
        keys[i * 64 : i * 64 + 64, :] = k.astype(jnp.bfloat16)
        v = recv_ref[32 + i, :CTX].reshape(64, 128).astype(jnp.float32)
        v = jnp.where(at0, v0, jnp.where(at1, v1, v))
        v = jnp.where(live, v, 0.0)
        vals[i * 64 : i * 64 + 64, :] = v.astype(jnp.bfloat16)
    scale = 1.0 / math.sqrt(HD)
    allowed = kpos_ref[...] <= qpos_ref[...]
    rowlive = lax.broadcasted_iota(jnp.int32, (64, 128), 0) < 2 * total
    for head in range(QH):
        q = q_ref[:, head * HD : head * HD + HD]
        s = lax.dot_general(
            q, keys[...], (((1,), (1,)), ((), ())),
            preferred_element_type=jnp.float32,
        )
        s = jnp.where(allowed, s * scale, -1e30)
        peak = jnp.max(s, axis=1, keepdims=True)
        w = jnp.exp(s - peak)
        norm = jnp.sum(w, axis=1, keepdims=True)
        mixed = jnp.dot(
            w.astype(jnp.bfloat16), vals[...], preferred_element_type=jnp.float32
        )
        out = jnp.where(rowlive, mixed / norm, 0.0)
        out_ref[:, head * HD : head * HD + HD] = out.astype(jnp.bfloat16)


def update_kernel(pos_ref, x_ref, rows_ref, out_ref):
    row = lax.broadcasted_iota(jnp.int32, (8, 128), 0)

    def step(l, carry):
        at0 = row == pos_ref[2 * l]
        at1 = row == pos_ref[2 * l + 1]
        for head in range(8):
            for kv in range(2):
                lanes = pl.ds(head * 256 + kv * 128, 128)
                pairf = rows_ref[head, l, kv].astype(jnp.float32)
                old = x_ref[l, :, lanes].astype(jnp.float32)
                new = jnp.where(at0, pairf[0:1], jnp.where(at1, pairf[1:2], old))
                out_ref[l, :, lanes] = new.astype(jnp.bfloat16)
        return carry

    lax.fori_loop(0, 16, step, 0)


def local(kv_cache, route, queries, fresh_kv, picked):
    own = lax.axis_index("inst").astype(jnp.int32)
    y = lax.axis_index("tp").astype(jnp.int32)
    me = jnp.stack([own, y])
    bf = jnp.bfloat16
    ctrl = jnp.concatenate([route, picked.reshape(64)]).astype(bf)
    ctrl = jnp.pad(ctrl[None, :], ((0, 1), (0, 48)))
    spread = pl.pallas_call(
        spread_kernel,
        out_shape=jax.ShapeDtypeStruct((512, 3, 2, 128), bf),
        in_specs=[SMEM, VMEM, VMEM],
        out_specs=VMEM,
        compiler_params=PARAMS,
        name="spread",
    )(me, kv_cache, ctrl)
    got = lax.all_to_all(
        spread, ("inst", "tp"), split_axis=0, concat_axis=0, tiled=True
    )

    half = HD // 2
    freqs = jnp.power(
        jnp.float32(THETA), -2.0 * jnp.arange(half, dtype=jnp.float32) / HD
    )
    shift = (jnp.arange(64, dtype=jnp.int32) // 2 * 64).astype(jnp.float32)
    angle = shift[:, None] * freqs[None, :]
    cos = jnp.cos(angle)
    sin = jnp.sin(angle)
    cos2 = jnp.concatenate([cos, cos], axis=1)
    sin2 = jnp.concatenate([-sin, sin], axis=1)

    fk = fresh_kv[:, :HD].astype(jnp.float32)
    swapped = jnp.concatenate([fk[:, half:], fk[:, :half]], axis=1)
    back_k = (fk * cos2 - swapped * sin2).astype(bf)
    back = jnp.stack(
        [back_k.reshape(32, 2, HD), fresh_kv[:, HD:].reshape(32, 2, HD)], axis=1
    )

    every = got.reshape(64, 8, 3, 2, 128)[:, 0, 2, 0, :]
    tab, slot = pl.pallas_call(
        tables_kernel,
        out_shape=(
            jax.ShapeDtypeStruct((64, 128), jnp.int32),
            jax.ShapeDtypeStruct((8, 128), jnp.int32),
        ),
        in_specs=[SMEM, VMEM],
        out_specs=(VMEM, VMEM),
        compiler_params=PARAMS,
        name="tables",
    )(me, every)
    send = pl.pallas_call(
        dispatch_kernel,
        out_shape=jax.ShapeDtypeStruct((64 * UNITS, 2, 128), bf),
        in_specs=[SMEM, SMEM, VMEM, VMEM],
        out_specs=VMEM,
        compiler_params=PARAMS,
        name="dispatch",
    )(me, tab, got, back)
    recv = lax.all_to_all(
        send.reshape(64, UNITS, 2, 128), "inst", split_axis=0, concat_axis=0,
        tiled=True,
    )

    mine = lax.dynamic_index_in_dim(tab, own, 0, keepdims=False)
    block_exec = route
    within = mine[32:48]
    rank = mine[48:64]
    units = recv.reshape(64, UNITS // 2, 2, 2, 128)
    rows = units[block_exec, CTX // 2 + within]
    rows = jnp.broadcast_to(rows[None], (8,) + rows.shape)
    rows = lax.all_to_all(rows, "tp", split_axis=0, concat_axis=0, tiled=True)
    picks = every[:, 16:80].reshape(64, 32, 2).astype(jnp.int32)
    pos = picks[block_exec, rank].reshape(32) - 8 * y
    updated = pl.pallas_call(
        update_kernel,
        out_shape=jax.ShapeDtypeStruct(kv_cache.shape, bf),
        in_specs=[SMEM, VMEM, VMEM],
        out_specs=VMEM,
        compiler_params=PARAMS,
        name="update",
    )(pos, kv_cache, rows)

    total = slot[1, :1]
    lj = slot[0, :32]
    g = jnp.arange(8, dtype=jnp.int32)[:, None, None, None]
    pair = jnp.arange(4, dtype=jnp.int32)[None, :, None, None]
    j = jnp.arange(32, dtype=jnp.int32)[None, None, :, None]
    r2 = jnp.arange(2, dtype=jnp.int32)
    kpos = j * 64 + ((g - lj[:, None]) & 7) * 8 + pair * 2 + r2
    kpos = jnp.where(j < total[0], kpos, 1 << 20).reshape(1, 2048)
    qpos = (jnp.arange(32, dtype=jnp.int32)[:, None] * 64 + picked).reshape(64, 1)
    unit = ((picked // 8 + lj[:, None]) & 7) * 4 + (picked & 7) // 2
    hit = (picked & 1)[:, None, :] == r2[None, :, None]
    where = jnp.where(hit, unit[:, None, :], -1).reshape(64, 2)
    i0 = jnp.broadcast_to(where[:, 0:1], (64, 128))
    i1 = jnp.broadcast_to(where[:, 1:2], (64, 128))
    fr = fresh_kv.reshape(32, 2, 256)
    f0 = jnp.repeat(fr[:, 0], 2, axis=0)
    f1 = jnp.repeat(fr[:, 1], 2, axis=0)
    attn_out = pl.pallas_call(
        attention_kernel,
        out_shape=jax.ShapeDtypeStruct(queries.shape, bf),
        in_specs=[SMEM] + [VMEM] * 10,
        out_specs=VMEM,
        scratch_shapes=[
            pltpu.VMEM((2048, HD), bf),
            pltpu.VMEM((2048, HD), bf),
        ],
        compiler_params=PARAMS,
        cost_estimate=pl.CostEstimate(
            flops=4 * 384 * 2048 * 128, bytes_accessed=1500000,
            transcendentals=384 * 2048,
        ),
        name="attend",
    )(total, recv, queries, f0, f1, i0, i1, cos2, sin2, kpos, qpos)
    return attn_out, updated


def solution(mesh):
    placed = (P("inst", "tp", None), P("inst"), P("inst", "tp"), P("inst", "tp"), P("inst", None))
    return jax.shard_map(
        local,
        mesh=mesh,
        in_specs=placed,
        out_specs=(P("inst", "tp"), P("inst", "tp", None)),
        check_vma=False,
    )
```

```python
import functools
import math

import jax
import jax.numpy as jnp
from jax import lax
from jax.experimental import pallas as pl
from jax.experimental.pallas import tpu as pltpu
from jax.sharding import PartitionSpec as P

HD = 128
QH = 6
THETA = 1000000.0
CTX = 32
UNITS = 36
VMEM = pl.BlockSpec(memory_space=pltpu.VMEM)
SMEM = pl.BlockSpec(memory_space=pltpu.SMEM)
PARAMS = pltpu.CompilerParams(vmem_limit_bytes=40 * 1024 * 1024)


def spread_kernel(x_ref, route_ref, picked_ref, out_ref):
    def step(block, carry):
        for head in range(8):
            for kv in range(2):
                lane = head * 256 + kv * 128
                for pair in range(4):
                    out_ref[head * 8 + kv * 4 + pair, block] = x_ref[
                        block, pl.ds(2 * pair, 2), pl.ds(lane, 128)
                    ]
        return carry

    lax.fori_loop(0, 16, step, 0)
    row = lax.broadcasted_iota(jnp.int32, (2, 128), 0)
    ctrl = jnp.where(row == 0, route_ref[...], picked_ref[...])
    ctrl = ctrl.astype(jnp.float32).astype(jnp.bfloat16)
    for d in range(64):
        out_ref[d, 16] = ctrl


def dispatch_kernel(own_ref, r_ref, back_ref, out_ref, tab_ref, tabs, sem):
    own = own_ref[0].astype(jnp.float32)
    ctrl = r_ref[:, 16, 0, :].astype(jnp.float32)
    lane = lax.broadcasted_iota(jnp.int32, (64, 128), 1)
    lanef = lane.astype(jnp.float32)
    routes = [ctrl[:, l : l + 1] for l in range(16)]
    masks = [jnp.where(r == lanef, 1.0, 0.0) for r in routes]
    counts = functools.reduce(lambda a, b: a + b, masks)
    row = lax.broadcasted_iota(jnp.int32, (64, 64), 0)
    col = lax.broadcasted_iota(jnp.int32, (64, 64), 1)
    lower = jnp.where(col < row, 1.0, 0.0).astype(jnp.bfloat16)
    starts = jnp.dot(
        lower, counts.astype(jnp.bfloat16), preferred_element_type=jnp.float32
    )
    tab = jnp.zeros((64, 128), jnp.float32)
    seen = jnp.zeros((64, 128), jnp.float32)
    for l in range(16):
        within = jnp.sum(masks[l] * seen, axis=1, keepdims=True)
        rank = jnp.sum(masks[l] * starts, axis=1, keepdims=True) + within
        seen = seen + masks[l]
        tab = jnp.where(lane == l, routes[l] * UNITS + rank, tab)
        tab = jnp.where(lane == 32 + l, within, tab)
        tab = jnp.where(lane == 48 + l, rank, tab)
    own_lane = lanef == own
    first = jnp.sum(jnp.where(own_lane, starts, 0.0), axis=1, keepdims=True)
    total = jnp.sum(jnp.where(own_lane, counts, 0.0))
    tab = jnp.where(lane == 16, first, tab)
    tab = jnp.where(lane == 17, total, tab)
    tab_ref[...] = tab.astype(jnp.int32)
    copy = pltpu.make_async_copy(tab_ref, tabs, sem)
    copy.start()
    copy.wait()

    def step(h, carry):
        place = [tabs[h, l] for l in range(16)]
        units = [r_ref[h, l] for l in range(16)]
        first = tabs[h, 16]
        slots = [jnp.minimum(first + s, CTX - 1) for s in range(2)]
        backs = [back_ref[slots[s], kv] for s in range(2) for kv in range(2)]
        for l in range(16):
            out_ref[place[l]] = units[l]
        for n in range(4):
            out_ref[h * UNITS + CTX + n] = backs[n]
        return carry

    lax.fori_loop(0, 64, step, 0, unroll=2)


def attention_kernel(
    total_ref, recv_ref, q_ref, f0_ref, f1_ref, i0_ref, i1_ref,
    cos_ref, sin_ref, qpos_ref, out_ref, keys, vals,
):
    total = total_ref[0]
    cos = cos_ref[...]
    sin = sin_ref[...]
    pick0 = i0_ref[...]
    pick1 = i1_ref[...]
    live = lax.broadcasted_iota(jnp.int32, (64, 128), 0) < 2 * total
    k0 = f0_ref[:, :128].astype(jnp.float32)
    k1 = f1_ref[:, :128].astype(jnp.float32)
    v0 = f0_ref[:, 128:].astype(jnp.float32)
    v1 = f1_ref[:, 128:].astype(jnp.float32)
    for i in range(32):
        at0 = pick0 == i
        at1 = pick1 == i
        src = i // 4 * 8 + i % 4
        k = recv_ref[src, : 2 * CTX, :].astype(jnp.float32)
        k = k * cos + pltpu.roll(k, 64, 1) * sin
        k = jnp.where(at0, k0, jnp.where(at1, k1, k))
        keys[i * 64 : i * 64 + 64, :] = k.astype(jnp.bfloat16)
        v = recv_ref[src + 4, : 2 * CTX, :].astype(jnp.float32)
        v = jnp.where(at0, v0, jnp.where(at1, v1, v))
        v = jnp.where(live, v, 0.0)
        vals[i * 64 : i * 64 + 64, :] = v.astype(jnp.bfloat16)
    scale = 1.0 / math.sqrt(HD)
    col = lax.broadcasted_iota(jnp.int32, (64, 2048), 1)
    kpos = (col & 63) // 2 * 64 + (col >> 6) * 2 + (col & 1)
    allowed = (kpos <= qpos_ref[...]) & (kpos < total * 64)
    rowlive = lax.broadcasted_iota(jnp.int32, (64, 128), 0) < 2 * total
    for head in range(QH):
        q = q_ref[:, head * HD : head * HD + HD]
        s = lax.dot_general(
            q, keys[...], (((1,), (1,)), ((), ())),
            preferred_element_type=jnp.float32,
        )
        s = jnp.where(allowed, s * scale, -1e30)
        peak = jnp.max(s, axis=1, keepdims=True)
        w = jnp.exp(s - peak)
        norm = jnp.sum(w, axis=1, keepdims=True)
        mixed = jnp.dot(
            w.astype(jnp.bfloat16), vals[...], preferred_element_type=jnp.float32
        )
        out = jnp.where(rowlive, mixed / norm, 0.0)
        out_ref[:, head * HD : head * HD + HD] = out.astype(jnp.bfloat16)


def update_kernel(pos_ref, x_ref, rows_ref, out_ref):
    row = lax.broadcasted_iota(jnp.int32, (8, 128), 0)

    def step(l, carry):
        at0 = row == pos_ref[2 * l]
        at1 = row == pos_ref[2 * l + 1]
        for head in range(8):
            for kv in range(2):
                lanes = pl.ds(head * 256 + kv * 128, 128)
                pairf = rows_ref[head, l, kv].astype(jnp.float32)
                old = x_ref[l, :, lanes].astype(jnp.float32)
                new = jnp.where(at0, pairf[0:1], jnp.where(at1, pairf[1:2], old))
                out_ref[l, :, lanes] = new.astype(jnp.bfloat16)
        return carry

    lax.fori_loop(0, 16, step, 0)


def local(kv_cache, route, queries, fresh_kv, picked):
    own = lax.axis_index("inst").astype(jnp.int32)
    y = lax.axis_index("tp").astype(jnp.int32)
    bf = jnp.bfloat16
    spread = pl.pallas_call(
        spread_kernel,
        out_shape=jax.ShapeDtypeStruct((64, 17, 2, 128), bf),
        in_specs=[VMEM, VMEM, VMEM],
        out_specs=VMEM,
        compiler_params=PARAMS,
        name="spread",
    )(
        kv_cache,
        jnp.pad(route, (0, 112))[None, :],
        jnp.pad(picked.reshape(64), (0, 64))[None, :],
    )
    got = lax.all_to_all(spread, "tp", split_axis=0, concat_axis=0, tiled=True)
    got = lax.all_to_all(got, "inst", split_axis=0, concat_axis=0, tiled=True)

    half = HD // 2
    freqs = jnp.power(
        jnp.float32(THETA), -2.0 * jnp.arange(half, dtype=jnp.float32) / HD
    )
    shift = (jnp.arange(64, dtype=jnp.int32) // 2 * 64).astype(jnp.float32)
    angle = shift[:, None] * freqs[None, :]
    cos = jnp.cos(angle)
    sin = jnp.sin(angle)
    cos2 = jnp.concatenate([cos, cos], axis=1)
    sin2 = jnp.concatenate([-sin, sin], axis=1)

    fk = fresh_kv[:, :HD].astype(jnp.float32)
    swapped = jnp.concatenate([fk[:, half:], fk[:, :half]], axis=1)
    back_k = (fk * cos2 - swapped * sin2).astype(bf)
    back = jnp.stack(
        [back_k.reshape(32, 2, HD), fresh_kv[:, HD:].reshape(32, 2, HD)], axis=1
    )

    send, tab = pl.pallas_call(
        dispatch_kernel,
        out_shape=(
            jax.ShapeDtypeStruct((64 * UNITS, 2, 128), bf),
            jax.ShapeDtypeStruct((64, 128), jnp.int32),
        ),
        in_specs=[SMEM, VMEM, VMEM],
        out_specs=(VMEM, VMEM),
        scratch_shapes=[pltpu.SMEM((64, 128), jnp.int32), pltpu.SemaphoreType.DMA],
        compiler_params=PARAMS,
        name="dispatch",
    )(own[None], got, back)
    recv = lax.all_to_all(
        send.reshape(64, UNITS, 2, 128), "inst", split_axis=0, concat_axis=0,
        tiled=True,
    )

    mine = lax.dynamic_index_in_dim(tab, own, 0, keepdims=False)
    units = recv.reshape(64, UNITS // 2, 2, 2, 128)
    rows = units[route, CTX // 2 + mine[32:48]]
    rows = jnp.broadcast_to(rows[None], (8,) + rows.shape)
    rows = lax.all_to_all(rows, "tp", split_axis=0, concat_axis=0, tiled=True)
    picks = got[:, 16, 1, :64].reshape(64, 32, 2).astype(jnp.int32)
    pos = picks[route, mine[48:64]].reshape(32) - 8 * y
    updated = pl.pallas_call(
        update_kernel,
        out_shape=jax.ShapeDtypeStruct(kv_cache.shape, bf),
        in_specs=[SMEM, VMEM, VMEM],
        out_specs=VMEM,
        compiler_params=PARAMS,
        name="update",
    )(pos, kv_cache, rows)

    r2 = jnp.arange(2, dtype=jnp.int32)
    qpos = (jnp.arange(32, dtype=jnp.int32)[:, None] * 64 + picked).reshape(64, 1)
    hit = (picked & 1)[:, None, :] == r2[None, :, None]
    where = jnp.where(hit, (picked // 2)[:, None, :], -1).reshape(64, 2)
    i0 = jnp.broadcast_to(where[:, 0:1], (64, 128))
    i1 = jnp.broadcast_to(where[:, 1:2], (64, 128))
    fr = fresh_kv.reshape(32, 2, 256)
    f0 = jnp.repeat(fr[:, 0], 2, axis=0)
    f1 = jnp.repeat(fr[:, 1], 2, axis=0)
    attn_out = pl.pallas_call(
        attention_kernel,
        out_shape=jax.ShapeDtypeStruct(queries.shape, bf),
        in_specs=[SMEM] + [VMEM] * 9,
        out_specs=VMEM,
        scratch_shapes=[
            pltpu.VMEM((2048, HD), bf),
            pltpu.VMEM((2048, HD), bf),
        ],
        compiler_params=PARAMS,
        cost_estimate=pl.CostEstimate(
            flops=4 * 384 * 2048 * 128, bytes_accessed=1500000,
            transcendentals=384 * 2048,
        ),
        name="attend",
    )(
        mine[17:18], recv.reshape(64, 2 * UNITS, 128), queries, f0, f1, i0, i1,
        cos2, sin2, qpos,
    )
    return attn_out, updated


def solution(mesh):
    placed = (P("inst", "tp", None), P("inst"), P("inst", "tp"), P("inst", "tp"), P("inst", None))
    return jax.shard_map(
        local,
        mesh=mesh,
        in_specs=placed,
        out_specs=(P("inst", "tp"), P("inst", "tp", None)),
        check_vma=False,
    )
```

```python
import functools
import math

import jax
import jax.numpy as jnp
from jax import lax
from jax.experimental import pallas as pl
from jax.experimental.pallas import tpu as pltpu
from jax.sharding import PartitionSpec as P

HD = 128
QH = 6
THETA = 1000000.0
CTX = 32
UNITS = 36
VMEM = pl.BlockSpec(memory_space=pltpu.VMEM)
SMEM = pl.BlockSpec(memory_space=pltpu.SMEM)
DISPATCH_SCRATCH = [
    pltpu.VMEM((24, 128), jnp.int32),
    pltpu.SMEM((24, 128), jnp.int32),
    pltpu.SemaphoreType.DMA,
]
ATTEND_SCRATCH = [
    pltpu.VMEM((2048, HD), jnp.bfloat16),
    pltpu.VMEM((2048, HD), jnp.bfloat16),
]
PARAMS = pltpu.CompilerParams(vmem_limit_bytes=40 * 1024 * 1024)


def spread_kernel(x_ref, route_ref, picked_ref, out_ref):
    lane = lax.broadcasted_iota(jnp.int32, (8, 128), 1)
    ctrl = jnp.zeros((8, 128), jnp.int32)
    picks = jnp.zeros((8, 128), jnp.int32)
    for l in range(16):
        ctrl = jnp.where(lane == l, route_ref[l], ctrl)
        ctrl = ctrl + jnp.where(lane == 64 + route_ref[l], 1, 0)
    for j in range(32):
        for w in range(2):
            picks = jnp.where(lane == 2 * j + w, picked_ref[j, w], picks)
    row = lax.broadcasted_iota(jnp.int32, (8, 128), 0)
    ctrl = jnp.where(row == 0, ctrl, picks)[:2]
    ctrl = ctrl.astype(jnp.float32).astype(jnp.bfloat16)
    for d in range(64):
        out_ref[d, 16] = ctrl

    def step(block, carry):
        for head in range(8):
            for kv in range(2):
                lane = head * 256 + kv * 128
                for pair in range(4):
                    out_ref[head * 8 + kv * 4 + pair, block] = x_ref[
                        block, pl.ds(2 * pair, 2), pl.ds(lane, 128)
                    ]
        return carry

    lax.fori_loop(0, 16, step, 0)


def dispatch_kernel(own_ref, r_ref, back_ref, out_ref, tab_ref, info_ref, packed, tabs, sem):
    own = own_ref[0]
    ctrl = r_ref[:, 16, 0, :].astype(jnp.float32)
    lane = lax.broadcasted_iota(jnp.int32, (64, 128), 1)
    counts = pltpu.roll(ctrl, 64, 1)
    row = lax.broadcasted_iota(jnp.int32, (64, 64), 0)
    col = lax.broadcasted_iota(jnp.int32, (64, 64), 1)
    lower = jnp.where(col < row, 1.0, 0.0).astype(jnp.bfloat16)
    starts = jnp.dot(
        lower, counts.astype(jnp.bfloat16), preferred_element_type=jnp.float32
    ).astype(jnp.int32)
    routes = jnp.where(lane < 16, ctrl, 0.0).astype(jnp.int32)
    within = jnp.zeros((64, 128), jnp.int32)
    for d in range(1, 16):
        same = (pltpu.roll(ctrl, d, 1) == ctrl) & (lane >= d)
        within = within + jnp.where(same, 1, 0)
    slot = jnp.take_along_axis(starts, routes, axis=1) + within
    place = routes * UNITS + slot
    ret = routes * UNITS + CTX + 2 * within
    tab_ref[...] = jnp.where(lane < 16, within, pltpu.roll(slot, 16, 1))
    own_lane = lane == own
    first = jnp.sum(jnp.where(own_lane, starts, 0), axis=1, keepdims=True)
    lane8 = lax.broadcasted_iota(jnp.int32, (8, 128), 1)
    for n, table in enumerate((place, ret, jnp.broadcast_to(first, (64, 128)))):
        acc = jnp.zeros((8, 128), jnp.int32)
        for a in range(8):
            part = table[8 * a : 8 * a + 8]
            if a:
                part = pltpu.roll(part, 16 * a, 1)
            acc = jnp.where(lane8 // 16 == a, part, acc)
        packed[8 * n : 8 * n + 8] = acc
    copy = pltpu.make_async_copy(packed, tabs, sem)
    copy.start()
    copy.wait()

    def step(a, carry):
        for r in range(8):
            h = a * 8 + r
            place = [tabs[r, a * 16 + l] for l in range(16)]
            units = [r_ref[h, l] for l in range(16)]
            first = tabs[16 + r, a * 16]
            slots = [jnp.minimum(first + s, CTX - 1) for s in range(2)]
            backs = [back_ref[slots[s], kv] for s in range(2) for kv in range(2)]
            for l in range(16):
                out_ref[place[l]] = units[l]
            for n in range(4):
                out_ref[h * UNITS + CTX + n] = backs[n]
        return carry

    lax.fori_loop(0, 8, step, 0)
    for l in range(16):
        info_ref[l] = tabs[8 + lax.rem(own, 8), own // 8 * 16 + l]
    info_ref[16] = jnp.sum(jnp.where(own_lane, counts, 0.0)).astype(jnp.int32)


def collect_kernel(info_ref, recv_ref, out_ref):
    for l in range(16):
        for kv in range(2):
            unit = recv_ref[info_ref[l] + kv]
            for t in range(8):
                out_ref[t * 32 + l * 2 + kv] = unit


def attention_kernel(
    info_ref, recv_ref, q_ref, f0_ref, f1_ref, i0_ref, i1_ref,
    cos_ref, sin_ref, qpos_ref, out_ref, keys, vals,
):
    total = info_ref[16]
    cos = cos_ref[...]
    sin = sin_ref[...]
    pick0 = i0_ref[...]
    pick1 = i1_ref[...]
    live = lax.broadcasted_iota(jnp.int32, (64, 128), 0) < 2 * total
    k0 = f0_ref[:, :128].astype(jnp.float32)
    k1 = f1_ref[:, :128].astype(jnp.float32)
    v0 = f0_ref[:, 128:].astype(jnp.float32)
    v1 = f1_ref[:, 128:].astype(jnp.float32)
    for i in range(32):
        at0 = pick0 == i
        at1 = pick1 == i
        src = i // 4 * 8 + i % 4
        k = recv_ref[src, : 2 * CTX, :].astype(jnp.float32)
        k = k * cos + pltpu.roll(k, 64, 1) * sin
        k = jnp.where(at0, k0, jnp.where(at1, k1, k))
        keys[i * 64 : i * 64 + 64, :] = k.astype(jnp.bfloat16)
        v = recv_ref[src + 4, : 2 * CTX, :].astype(jnp.float32)
        v = jnp.where(at0, v0, jnp.where(at1, v1, v))
        v = jnp.where(live, v, 0.0)
        vals[i * 64 : i * 64 + 64, :] = v.astype(jnp.bfloat16)
    col = lax.broadcasted_iota(jnp.int32, (64, 2048), 1)
    kpos = (col & 63) // 2 * 64 + (col >> 6) * 2 + (col & 1)
    allowed = (kpos <= qpos_ref[...]) & (kpos < total * 64)
    rowlive = lax.broadcasted_iota(jnp.int32, (64, 128), 0) < 2 * total
    factor = math.log2(math.e) / math.sqrt(HD)
    group = 3
    for base in range(0, QH, group):
        heads = range(base, base + group)
        q = jnp.concatenate([q_ref[:, h * HD : h * HD + HD] for h in heads], axis=0)
        s = lax.dot_general(
            q, keys[...], (((1,), (1,)), ((), ())),
            preferred_element_type=jnp.float32,
        )
        s = jnp.where(allowed[None], s.reshape(group, 64, 2048), -1e30)
        peak = jnp.max(s, axis=2, keepdims=True)
        w = jnp.exp2((s - peak) * factor)
        norm = jnp.sum(w, axis=2, keepdims=True)
        mixed = jnp.dot(
            w.astype(jnp.bfloat16).reshape(group * 64, 2048), vals[...],
            preferred_element_type=jnp.float32,
        ).reshape(group, 64, HD)
        out = jnp.where(rowlive[None], mixed / norm, 0.0)
        for n, h in enumerate(heads):
            out_ref[:, h * HD : h * HD + HD] = out[n].astype(jnp.bfloat16)


def update_kernel(pos_ref, x_ref, rows_ref, out_ref):
    row = lax.broadcasted_iota(jnp.int32, (8, 128), 0)

    def step(l, carry):
        at0 = row == pos_ref[2 * l]
        at1 = row == pos_ref[2 * l + 1]
        for head in range(8):
            for kv in range(2):
                lanes = pl.ds(head * 256 + kv * 128, 128)
                pairf = rows_ref[head, l, kv].astype(jnp.float32)
                old = x_ref[l, :, lanes].astype(jnp.float32)
                new = jnp.where(at0, pairf[0:1], jnp.where(at1, pairf[1:2], old))
                out_ref[l, :, lanes] = new.astype(jnp.bfloat16)
        return carry

    lax.fori_loop(0, 16, step, 0)


def local(kv_cache, route, queries, fresh_kv, picked):
    own = lax.axis_index("inst").astype(jnp.int32)
    y = lax.axis_index("tp").astype(jnp.int32)
    bf = jnp.bfloat16
    spread = pl.pallas_call(
        spread_kernel,
        out_shape=jax.ShapeDtypeStruct((64, 17, 2, 128), bf),
        in_specs=[VMEM, SMEM, SMEM],
        out_specs=VMEM,
        compiler_params=PARAMS,
        name="spread",
    )(kv_cache, route, picked)
    got = lax.all_to_all(spread, "tp", split_axis=0, concat_axis=0, tiled=True)
    got = lax.all_to_all(got, "inst", split_axis=0, concat_axis=0, tiled=True)

    half = HD // 2
    freqs = jnp.power(
        jnp.float32(THETA), -2.0 * jnp.arange(half, dtype=jnp.float32) / HD
    )
    shift = (jnp.arange(64, dtype=jnp.int32) // 2 * 64).astype(jnp.float32)
    angle = shift[:, None] * freqs[None, :]
    cos = jnp.cos(angle)
    sin = jnp.sin(angle)
    cos2 = jnp.concatenate([cos, cos], axis=1)
    sin2 = jnp.concatenate([-sin, sin], axis=1)

    fk = fresh_kv[:, :HD].astype(jnp.float32)
    swapped = jnp.concatenate([fk[:, half:], fk[:, :half]], axis=1)
    back_k = (fk * cos2 - swapped * sin2).astype(bf)
    back = jnp.stack(
        [back_k.reshape(32, 2, HD), fresh_kv[:, HD:].reshape(32, 2, HD)], axis=1
    )

    send, tab, info = pl.pallas_call(
        dispatch_kernel,
        out_shape=(
            jax.ShapeDtypeStruct((64 * UNITS, 2, 128), bf),
            jax.ShapeDtypeStruct((64, 128), jnp.int32),
            jax.ShapeDtypeStruct((32,), jnp.int32),
        ),
        in_specs=[SMEM, VMEM, VMEM],
        out_specs=(VMEM, VMEM, SMEM),
        scratch_shapes=DISPATCH_SCRATCH,
        compiler_params=PARAMS,
        name="dispatch",
    )(own[None], got, back)
    recv = lax.all_to_all(
        send.reshape(64, UNITS, 2, 128), "inst", split_axis=0, concat_axis=0,
        tiled=True,
    )

    mine = lax.dynamic_index_in_dim(tab, own, 0, keepdims=False)
    rows = pl.pallas_call(
        collect_kernel,
        out_shape=jax.ShapeDtypeStruct((256, 2, 128), bf),
        in_specs=[SMEM, VMEM],
        out_specs=VMEM,
        compiler_params=PARAMS,
        name="collect",
    )(info, recv.reshape(64 * UNITS, 2, 128)).reshape(8, 16, 2, 2, 128)
    rows = lax.all_to_all(rows, "tp", split_axis=0, concat_axis=0, tiled=True)
    picks = got[:, 16, 1, :64].reshape(64, 32, 2).astype(jnp.int32)
    pos = picks[route, mine[16:32]].reshape(32) - 8 * y
    updated = pl.pallas_call(
        update_kernel,
        out_shape=jax.ShapeDtypeStruct(kv_cache.shape, bf),
        in_specs=[SMEM, VMEM, VMEM],
        out_specs=VMEM,
        compiler_params=PARAMS,
        name="update",
    )(pos, kv_cache, rows)

    r2 = jnp.arange(2, dtype=jnp.int32)
    qpos = (jnp.arange(32, dtype=jnp.int32)[:, None] * 64 + picked).reshape(64, 1)
    hit = (picked & 1)[:, None, :] == r2[None, :, None]
    where = jnp.where(hit, (picked // 2)[:, None, :], -1).reshape(64, 2)
    i0 = jnp.broadcast_to(where[:, 0:1], (64, 128))
    i1 = jnp.broadcast_to(where[:, 1:2], (64, 128))
    fr = fresh_kv.reshape(32, 2, 256)
    f0 = jnp.repeat(fr[:, 0], 2, axis=0)
    f1 = jnp.repeat(fr[:, 1], 2, axis=0)
    attn_out = pl.pallas_call(
        attention_kernel,
        out_shape=jax.ShapeDtypeStruct(queries.shape, bf),
        in_specs=[SMEM] + [VMEM] * 9,
        out_specs=VMEM,
        scratch_shapes=ATTEND_SCRATCH,
        compiler_params=PARAMS,
        cost_estimate=pl.CostEstimate(
            flops=4 * 384 * 2048 * 128, bytes_accessed=1500000,
            transcendentals=384 * 2048,
        ),
        name="attend",
    )(
        info, recv.reshape(64, 2 * UNITS, 128), queries, f0, f1, i0, i1,
        cos2, sin2, qpos,
    )
    return attn_out, updated


def solution(mesh):
    placed = (P("inst", "tp", None), P("inst"), P("inst", "tp"), P("inst", "tp"), P("inst", None))
    return jax.shard_map(
        local,
        mesh=mesh,
        in_specs=placed,
        out_specs=(P("inst", "tp"), P("inst", "tp", None)),
        check_vma=False,
    )
```

```python
import functools
import math

import jax
import jax.numpy as jnp
from jax import lax
from jax.experimental import pallas as pl
from jax.experimental.pallas import tpu as pltpu
from jax.sharding import PartitionSpec as P

HD = 128
QH = 6
THETA = 1000000.0
CTX = 32
UNITS = 36
VMEM = pl.BlockSpec(memory_space=pltpu.VMEM)
SMEM = pl.BlockSpec(memory_space=pltpu.SMEM)
DISPATCH_SCRATCH = [
    pltpu.VMEM((8, 128), jnp.int32),
    pltpu.SMEM((8, 128), jnp.int32),
    pltpu.SemaphoreType.DMA,
]
ATTEND_SCRATCH = [
    pltpu.VMEM((2048, HD), jnp.bfloat16),
    pltpu.VMEM((2048, HD), jnp.bfloat16),
]
PARAMS = pltpu.CompilerParams(vmem_limit_bytes=40 * 1024 * 1024)


def spread_kernel(x_ref, route_ref, picked_ref, out_ref):
    lane = lax.broadcasted_iota(jnp.int32, (2, 128), 1)
    ctrl = jnp.zeros((2, 128), jnp.int32)
    for l in range(16):
        ctrl = jnp.where(lane == l, route_ref[l], ctrl)
        ctrl = ctrl + jnp.where(lane == 64 + route_ref[l], 1, 0)
    picks = jnp.concatenate(
        [picked_ref[0:1, :], picked_ref[1:2, :], jnp.zeros((1, 64), jnp.int32)], axis=1
    )
    row = lax.broadcasted_iota(jnp.int32, (2, 128), 0)
    ctrl = jnp.where(row == 0, ctrl, picks)
    ctrl = ctrl.astype(jnp.float32).astype(jnp.bfloat16)
    for d in range(64):
        out_ref[d, 16] = ctrl

    def step(block, carry):
        for head in range(8):
            for kv in range(2):
                lane = head * 256 + kv * 128
                for pair in range(4):
                    out_ref[head * 8 + kv * 4 + pair, block] = x_ref[
                        block, pl.ds(2 * pair, 2), pl.ds(lane, 128)
                    ]
        return carry

    lax.fori_loop(0, 16, step, 0)


def dispatch_kernel(own_ref, r_ref, back_ref, out_ref, tab_ref, total_ref, packed, tabs, sem):
    own = own_ref[0]
    ctrl = r_ref[:, 16, 0, :].astype(jnp.float32)
    lane = lax.broadcasted_iota(jnp.int32, (64, 128), 1)
    counts = pltpu.roll(ctrl, 64, 1)
    row = lax.broadcasted_iota(jnp.int32, (64, 64), 0)
    col = lax.broadcasted_iota(jnp.int32, (64, 64), 1)
    lower = jnp.where(col < row, 1.0, 0.0).astype(jnp.bfloat16)
    starts = jnp.dot(
        lower, counts.astype(jnp.bfloat16), preferred_element_type=jnp.float32
    ).astype(jnp.int32)
    routes = jnp.where(lane < 16, ctrl, 0.0).astype(jnp.int32)
    within = jnp.zeros((64, 128), jnp.int32)
    for d in range(1, 16):
        same = (pltpu.roll(ctrl, d, 1) == ctrl) & (lane >= d)
        within = within + jnp.where(same, 1, 0)
    slot = jnp.take_along_axis(starts, routes, axis=1) + within
    place = routes * UNITS + slot
    ret = routes * UNITS + CTX + 2 * within
    tab_ref[...] = jnp.where(lane < 16, ret, pltpu.roll(slot, 16, 1))
    own_lane = lane == own
    first = jnp.sum(jnp.where(own_lane, starts, 0), axis=1, keepdims=True)
    table = place + 4096 * first
    lane8 = lax.broadcasted_iota(jnp.int32, (8, 128), 1)
    acc = jnp.zeros((8, 128), jnp.int32)
    for a in range(8):
        part = table[8 * a : 8 * a + 8]
        if a:
            part = pltpu.roll(part, 16 * a, 1)
        acc = jnp.where(lane8 // 16 == a, part, acc)
    packed[...] = acc
    copy = pltpu.make_async_copy(packed, tabs, sem)
    copy.start()
    total = jnp.sum(jnp.where(own_lane, counts, 0.0)).astype(jnp.int32)
    total_ref[...] = jnp.full((1, 128), total, jnp.int32)
    copy.wait()

    def step(a, carry):
        for r in range(8):
            h = a * 8 + r
            both = [tabs[r, a * 16 + l] for l in range(16)]
            place = [v & 4095 for v in both]
            units = [r_ref[h, l] for l in range(16)]
            first = both[0] >> 12
            slots = [jnp.minimum(first + s, CTX - 1) for s in range(2)]
            backs = [back_ref[slots[s], kv] for s in range(2) for kv in range(2)]
            for l in range(16):
                out_ref[place[l]] = units[l]
            for n in range(4):
                out_ref[h * UNITS + CTX + n] = backs[n]
        return carry

    lax.fori_loop(0, 8, step, 0)


def collect_kernel(info_ref, recv_ref, out_ref):
    for l in range(16):
        for kv in range(2):
            unit = recv_ref[info_ref[l] + kv]
            for t in range(8):
                out_ref[t * 32 + l * 2 + kv] = unit


def attention_kernel(
    total_ref, recv_ref, q_ref, f0_ref, f1_ref, i0_ref, i1_ref,
    cos_ref, sin_ref, qpos_ref, out_ref, keys, vals,
):
    total = total_ref[0]
    cos = cos_ref[...]
    sin = sin_ref[...]
    pick0 = i0_ref[...]
    pick1 = i1_ref[...]
    live = lax.broadcasted_iota(jnp.int32, (64, 128), 0) < 2 * total
    k0 = f0_ref[:, :128].astype(jnp.float32)
    k1 = f1_ref[:, :128].astype(jnp.float32)
    v0 = f0_ref[:, 128:].astype(jnp.float32)
    v1 = f1_ref[:, 128:].astype(jnp.float32)
    for i in range(32):
        at0 = pick0 == i
        at1 = pick1 == i
        src = i // 4 * 8 + i % 4
        k = recv_ref[src, : 2 * CTX, :].astype(jnp.float32)
        k = k * cos + pltpu.roll(k, 64, 1) * sin
        k = jnp.where(at0, k0, jnp.where(at1, k1, k))
        keys[i * 64 : i * 64 + 64, :] = k.astype(jnp.bfloat16)
        v = recv_ref[src + 4, : 2 * CTX, :].astype(jnp.float32)
        v = jnp.where(at0, v0, jnp.where(at1, v1, v))
        v = jnp.where(live, v, 0.0)
        vals[i * 64 : i * 64 + 64, :] = v.astype(jnp.bfloat16)
    col = lax.broadcasted_iota(jnp.int32, (64, 2048), 1)
    kpos = (col & 63) // 2 * 64 + (col >> 6) * 2 + (col & 1)
    allowed = (kpos <= qpos_ref[...]) & (kpos < total * 64)
    rowlive = lax.broadcasted_iota(jnp.int32, (64, 128), 0) < 2 * total
    factor = math.log2(math.e) / math.sqrt(HD)
    group = 3
    for base in range(0, QH, group):
        heads = range(base, base + group)
        q = jnp.concatenate([q_ref[:, h * HD : h * HD + HD] for h in heads], axis=0)
        s = lax.dot_general(
            q, keys[...], (((1,), (1,)), ((), ())),
            preferred_element_type=jnp.float32,
        )
        s = jnp.where(allowed[None], s.reshape(group, 64, 2048), -1e30)
        peak = jnp.max(s, axis=2, keepdims=True)
        w = jnp.exp2((s - peak) * factor)
        norm = jnp.sum(w, axis=2, keepdims=True)
        mixed = jnp.dot(
            w.astype(jnp.bfloat16).reshape(group * 64, 2048), vals[...],
            preferred_element_type=jnp.float32,
        ).reshape(group, 64, HD)
        out = jnp.where(rowlive[None], mixed / norm, 0.0)
        for n, h in enumerate(heads):
            out_ref[:, h * HD : h * HD + HD] = out[n].astype(jnp.bfloat16)


def update_kernel(pos_ref, x_ref, rows_ref, out_ref):
    row = lax.broadcasted_iota(jnp.int32, (8, 128), 0)

    def step(l, carry):
        at0 = row == pos_ref[2 * l]
        at1 = row == pos_ref[2 * l + 1]
        for head in range(8):
            for kv in range(2):
                lanes = pl.ds(head * 256 + kv * 128, 128)
                pairf = rows_ref[head, l, kv].astype(jnp.float32)
                old = x_ref[l, :, lanes].astype(jnp.float32)
                new = jnp.where(at0, pairf[0:1], jnp.where(at1, pairf[1:2], old))
                out_ref[l, :, lanes] = new.astype(jnp.bfloat16)
        return carry

    lax.fori_loop(0, 16, step, 0)


def local(kv_cache, route, queries, fresh_kv, picked):
    own = lax.axis_index("inst").astype(jnp.int32)
    y = lax.axis_index("tp").astype(jnp.int32)
    bf = jnp.bfloat16
    spread = pl.pallas_call(
        spread_kernel,
        out_shape=jax.ShapeDtypeStruct((64, 17, 2, 128), bf),
        in_specs=[VMEM, SMEM, VMEM],
        out_specs=VMEM,
        compiler_params=PARAMS,
        name="spread",
    )(kv_cache, route, picked.T)
    got = lax.all_to_all(spread, "tp", split_axis=0, concat_axis=0, tiled=True)
    got = lax.all_to_all(got, "inst", split_axis=0, concat_axis=0, tiled=True)

    half = HD // 2
    freqs = jnp.power(
        jnp.float32(THETA), -2.0 * jnp.arange(half, dtype=jnp.float32) / HD
    )
    shift = (jnp.arange(64, dtype=jnp.int32) // 2 * 64).astype(jnp.float32)
    angle = shift[:, None] * freqs[None, :]
    cos = jnp.cos(angle)
    sin = jnp.sin(angle)
    cos2 = jnp.concatenate([cos, cos], axis=1)
    sin2 = jnp.concatenate([-sin, sin], axis=1)

    fk = fresh_kv[:, :HD].astype(jnp.float32)
    swapped = jnp.concatenate([fk[:, half:], fk[:, :half]], axis=1)
    back_k = (fk * cos2 - swapped * sin2).astype(bf)
    back = jnp.stack(
        [back_k.reshape(32, 2, HD), fresh_kv[:, HD:].reshape(32, 2, HD)], axis=1
    )

    send, tab, total = pl.pallas_call(
        dispatch_kernel,
        out_shape=(
            jax.ShapeDtypeStruct((64 * UNITS, 2, 128), bf),
            jax.ShapeDtypeStruct((64, 128), jnp.int32),
            jax.ShapeDtypeStruct((1, 128), jnp.int32),
        ),
        in_specs=[SMEM, VMEM, VMEM],
        out_specs=(VMEM, VMEM, VMEM),
        scratch_shapes=DISPATCH_SCRATCH,
        compiler_params=PARAMS,
        name="dispatch",
    )(own[None], got, back)
    recv = lax.all_to_all(
        send.reshape(64, UNITS, 2, 128), "inst", split_axis=0, concat_axis=0,
        tiled=True,
    )

    mine = lax.dynamic_index_in_dim(tab, own, 0, keepdims=False)
    rows = pl.pallas_call(
        collect_kernel,
        out_shape=jax.ShapeDtypeStruct((256, 2, 128), bf),
        in_specs=[SMEM, VMEM],
        out_specs=VMEM,
        compiler_params=PARAMS,
        name="collect",
    )(mine[:16], recv.reshape(64 * UNITS, 2, 128)).reshape(8, 16, 2, 2, 128)
    rows = lax.all_to_all(rows, "tp", split_axis=0, concat_axis=0, tiled=True)
    picks = got[:, 16, 1, :64].reshape(64, 2, 32).astype(jnp.int32)
    pos = picks[route, :, mine[16:32]].reshape(32) - 8 * y
    updated = pl.pallas_call(
        update_kernel,
        out_shape=jax.ShapeDtypeStruct(kv_cache.shape, bf),
        in_specs=[SMEM, VMEM, VMEM],
        out_specs=VMEM,
        compiler_params=PARAMS,
        name="update",
    )(pos, kv_cache, rows)

    r2 = jnp.arange(2, dtype=jnp.int32)
    qpos = (jnp.arange(32, dtype=jnp.int32)[:, None] * 64 + picked).reshape(64, 1)
    hit = (picked & 1)[:, None, :] == r2[None, :, None]
    where = jnp.where(hit, (picked // 2)[:, None, :], -1).reshape(64, 2)
    i0 = jnp.broadcast_to(where[:, 0:1], (64, 128))
    i1 = jnp.broadcast_to(where[:, 1:2], (64, 128))
    fr = fresh_kv.reshape(32, 2, 256)
    f0 = jnp.repeat(fr[:, 0], 2, axis=0)
    f1 = jnp.repeat(fr[:, 1], 2, axis=0)
    attn_out = pl.pallas_call(
        attention_kernel,
        out_shape=jax.ShapeDtypeStruct(queries.shape, bf),
        in_specs=[SMEM] + [VMEM] * 9,
        out_specs=VMEM,
        scratch_shapes=ATTEND_SCRATCH,
        compiler_params=PARAMS,
        cost_estimate=pl.CostEstimate(
            flops=4 * 384 * 2048 * 128, bytes_accessed=1500000,
            transcendentals=384 * 2048,
        ),
        name="attend",
    )(
        total[0, :1], recv.reshape(64, 2 * UNITS, 128), queries, f0, f1, i0, i1,
        cos2, sin2, qpos,
    )
    return attn_out, updated


def solution(mesh):
    placed = (P("inst", "tp", None), P("inst"), P("inst", "tp"), P("inst", "tp"), P("inst", None))
    return jax.shard_map(
        local,
        mesh=mesh,
        in_specs=placed,
        out_specs=(P("inst", "tp"), P("inst", "tp", None)),
        check_vma=False,
    )
```

```python
import functools
import math

import jax
import jax.numpy as jnp
from jax import lax
from jax.experimental import pallas as pl
from jax.experimental.pallas import tpu as pltpu
from jax.sharding import PartitionSpec as P

HD = 128
QH = 6
THETA = 1000000.0
CTX = 32
UNITS = 36
VMEM = pl.BlockSpec(memory_space=pltpu.VMEM)
SMEM = pl.BlockSpec(memory_space=pltpu.SMEM)
DISPATCH_SCRATCH = [
    pltpu.VMEM((8, 128), jnp.int32),
    pltpu.SMEM((8, 128), jnp.int32),
    pltpu.SemaphoreType.DMA,
]
ATTEND_SCRATCH = [
    pltpu.VMEM((2048, HD), jnp.bfloat16),
    pltpu.VMEM((2048, HD), jnp.bfloat16),
]
WHOLE = pltpu.CompilerParams(vmem_limit_bytes=66_400_000)
PARAMS = pltpu.CompilerParams(vmem_limit_bytes=40 * 1024 * 1024)


def spread_kernel(x_ref, route_ref, picked_ref, out_ref):
    lane = lax.broadcasted_iota(jnp.int32, (2, 128), 1)
    ctrl = jnp.zeros((2, 128), jnp.int32)
    for l in range(16):
        ctrl = jnp.where(lane == l, route_ref[l], ctrl)
        ctrl = ctrl + jnp.where(lane == 64 + route_ref[l], 1, 0)
    picks = jnp.concatenate(
        [picked_ref[0:1, :], picked_ref[1:2, :], jnp.zeros((1, 64), jnp.int32)], axis=1
    )
    row = lax.broadcasted_iota(jnp.int32, (2, 128), 0)
    ctrl = jnp.where(row == 0, ctrl, picks)
    ctrl = ctrl.astype(jnp.float32).astype(jnp.bfloat16)
    for d in range(64):
        out_ref[d, 16] = ctrl

    def step(block, carry):
        for head in range(8):
            for kv in range(2):
                lane = head * 256 + kv * 128
                for pair in range(4):
                    out_ref[head * 8 + kv * 4 + pair, block] = x_ref[
                        block, pl.ds(2 * pair, 2), pl.ds(lane, 128)
                    ]
        return carry

    lax.fori_loop(0, 16, step, 0)


def dispatch_kernel(own_ref, r_ref, back_ref, out_ref, tab_ref, total_ref, packed, tabs, sem):
    own = own_ref[0]
    ctrl = r_ref[:, 16, 0, :].astype(jnp.float32)
    lane = lax.broadcasted_iota(jnp.int32, (64, 128), 1)
    counts = pltpu.roll(ctrl, 64, 1)
    row = lax.broadcasted_iota(jnp.int32, (64, 64), 0)
    col = lax.broadcasted_iota(jnp.int32, (64, 64), 1)
    lower = jnp.where(col < row, 1.0, 0.0).astype(jnp.bfloat16)
    starts = jnp.dot(
        lower, counts.astype(jnp.bfloat16), preferred_element_type=jnp.float32
    ).astype(jnp.int32)
    routes = jnp.where(lane < 16, ctrl, 0.0).astype(jnp.int32)
    within = jnp.zeros((64, 128), jnp.int32)
    for d in range(1, 16):
        same = (pltpu.roll(ctrl, d, 1) == ctrl) & (lane >= d)
        within = within + jnp.where(same, 1, 0)
    slot = jnp.take_along_axis(starts, routes, axis=1) + within
    place = routes * UNITS + slot
    ret = routes * UNITS + CTX + 2 * within
    tab_ref[...] = jnp.where(lane < 16, ret, pltpu.roll(slot, 16, 1))
    own_lane = lane == own
    first = jnp.sum(jnp.where(own_lane, starts, 0), axis=1, keepdims=True)
    table = place + 4096 * first
    lane8 = lax.broadcasted_iota(jnp.int32, (8, 128), 1)
    acc = jnp.zeros((8, 128), jnp.int32)
    for a in range(8):
        part = table[8 * a : 8 * a + 8]
        if a:
            part = pltpu.roll(part, 16 * a, 1)
        acc = jnp.where(lane8 // 16 == a, part, acc)
    packed[...] = acc
    copy = pltpu.make_async_copy(packed, tabs, sem)
    copy.start()
    total = jnp.sum(jnp.where(own_lane, counts, 0.0)).astype(jnp.int32)
    total_ref[...] = jnp.full((1, 128), total, jnp.int32)
    copy.wait()

    def step(a, carry):
        for r in range(8):
            h = a * 8 + r
            both = [tabs[r, a * 16 + l] for l in range(16)]
            place = [v & 4095 for v in both]
            units = [r_ref[h, l] for l in range(16)]
            first = both[0] >> 12
            slots = [jnp.minimum(first + s, CTX - 1) for s in range(2)]
            backs = [back_ref[slots[s], kv] for s in range(2) for kv in range(2)]
            for l in range(16):
                out_ref[place[l]] = units[l]
            for n in range(4):
                out_ref[h * UNITS + CTX + n] = backs[n]
        return carry

    lax.fori_loop(0, 8, step, 0)


def collect_kernel(info_ref, recv_ref, out_ref):
    for l in range(16):
        for kv in range(2):
            unit = recv_ref[info_ref[l] + kv]
            for t in range(8):
                out_ref[t * 32 + l * 2 + kv] = unit


def attention_kernel(
    total_ref, recv_ref, q_ref, f0_ref, f1_ref, i0_ref, i1_ref,
    cos_ref, sin_ref, qpos_ref, out_ref, keys, vals,
):
    total = total_ref[0]
    cos = cos_ref[...]
    sin = sin_ref[...]
    pick0 = i0_ref[...]
    pick1 = i1_ref[...]
    live = lax.broadcasted_iota(jnp.int32, (64, 128), 0) < 2 * total
    k0 = f0_ref[:, :128].astype(jnp.float32)
    k1 = f1_ref[:, :128].astype(jnp.float32)
    v0 = f0_ref[:, 128:].astype(jnp.float32)
    v1 = f1_ref[:, 128:].astype(jnp.float32)
    for i in range(32):
        at0 = pick0 == i
        at1 = pick1 == i
        src = i // 4 * 8 + i % 4
        k = recv_ref[src, : 2 * CTX, :].astype(jnp.float32)
        k = k * cos + pltpu.roll(k, 64, 1) * sin
        k = jnp.where(at0, k0, jnp.where(at1, k1, k))
        keys[i * 64 : i * 64 + 64, :] = k.astype(jnp.bfloat16)
        v = recv_ref[src + 4, : 2 * CTX, :].astype(jnp.float32)
        v = jnp.where(at0, v0, jnp.where(at1, v1, v))
        v = jnp.where(live, v, 0.0)
        vals[i * 64 : i * 64 + 64, :] = v.astype(jnp.bfloat16)
    col = lax.broadcasted_iota(jnp.int32, (64, 2048), 1)
    kpos = (col & 63) // 2 * 64 + (col >> 6) * 2 + (col & 1)
    allowed = (kpos <= qpos_ref[...]) & (kpos < total * 64)
    rowlive = lax.broadcasted_iota(jnp.int32, (64, 128), 0) < 2 * total
    factor = math.log2(math.e) / math.sqrt(HD)
    group = 3
    for base in range(0, QH, group):
        heads = range(base, base + group)
        q = jnp.concatenate([q_ref[:, h * HD : h * HD + HD] for h in heads], axis=0)
        s = lax.dot_general(
            q, keys[...], (((1,), (1,)), ((), ())),
            preferred_element_type=jnp.float32,
        )
        s = jnp.where(allowed[None], s.reshape(group, 64, 2048), -1e30)
        peak = jnp.max(s, axis=2, keepdims=True)
        w = jnp.exp2((s - peak) * factor)
        norm = jnp.sum(w, axis=2, keepdims=True)
        mixed = jnp.dot(
            w.astype(jnp.bfloat16).reshape(group * 64, 2048), vals[...],
            preferred_element_type=jnp.float32,
        ).reshape(group, 64, HD)
        out = jnp.where(rowlive[None], mixed / norm, 0.0)
        for n, h in enumerate(heads):
            out_ref[:, h * HD : h * HD + HD] = out[n].astype(jnp.bfloat16)


def update_kernel(pos_ref, x_ref, rows_ref, out_ref):
    row = lax.broadcasted_iota(jnp.int32, (8, 128), 0)

    def step(l, carry):
        at0 = row == pos_ref[2 * l]
        at1 = row == pos_ref[2 * l + 1]
        for head in range(8):
            for kv in range(2):
                lanes = pl.ds(head * 256 + kv * 128, 128)
                pairf = rows_ref[head, l, kv].astype(jnp.float32)
                old = x_ref[l, :, lanes].astype(jnp.float32)
                new = jnp.where(at0, pairf[0:1], jnp.where(at1, pairf[1:2], old))
                out_ref[l, :, lanes] = new.astype(jnp.bfloat16)
        return carry

    lax.fori_loop(0, 16, step, 0)


def local(kv_cache, route, queries, fresh_kv, picked):
    own = lax.axis_index("inst").astype(jnp.int32)
    y = lax.axis_index("tp").astype(jnp.int32)
    bf = jnp.bfloat16
    spread = pl.pallas_call(
        spread_kernel,
        out_shape=jax.ShapeDtypeStruct((64, 17, 2, 128), bf),
        in_specs=[VMEM, SMEM, VMEM],
        out_specs=VMEM,
        compiler_params=WHOLE,
        name="spread",
    )(kv_cache, route, picked.T)
    got = lax.all_to_all(spread, "tp", split_axis=0, concat_axis=0, tiled=True)
    got = lax.all_to_all(got, "inst", split_axis=0, concat_axis=0, tiled=True)

    half = HD // 2
    freqs = jnp.power(
        jnp.float32(THETA), -2.0 * jnp.arange(half, dtype=jnp.float32) / HD
    )
    shift = (jnp.arange(64, dtype=jnp.int32) // 2 * 64).astype(jnp.float32)
    angle = shift[:, None] * freqs[None, :]
    cos = jnp.cos(angle)
    sin = jnp.sin(angle)
    cos2 = jnp.concatenate([cos, cos], axis=1)
    sin2 = jnp.concatenate([-sin, sin], axis=1)

    fk = fresh_kv[:, :HD].astype(jnp.float32)
    swapped = jnp.concatenate([fk[:, half:], fk[:, :half]], axis=1)
    back_k = (fk * cos2 - swapped * sin2).astype(bf)
    back = jnp.stack(
        [back_k.reshape(32, 2, HD), fresh_kv[:, HD:].reshape(32, 2, HD)], axis=1
    )

    send, tab, total = pl.pallas_call(
        dispatch_kernel,
        out_shape=(
            jax.ShapeDtypeStruct((64 * UNITS, 2, 128), bf),
            jax.ShapeDtypeStruct((64, 128), jnp.int32),
            jax.ShapeDtypeStruct((1, 128), jnp.int32),
        ),
        in_specs=[SMEM, VMEM, VMEM],
        out_specs=(VMEM, VMEM, VMEM),
        scratch_shapes=DISPATCH_SCRATCH,
        compiler_params=PARAMS,
        name="dispatch",
    )(own[None], got, back)
    recv = lax.all_to_all(
        send.reshape(64, UNITS, 2, 128), "inst", split_axis=0, concat_axis=0,
        tiled=True,
    )

    mine = lax.dynamic_index_in_dim(tab, own, 0, keepdims=False)
    rows = pl.pallas_call(
        collect_kernel,
        out_shape=jax.ShapeDtypeStruct((256, 2, 128), bf),
        in_specs=[SMEM, VMEM],
        out_specs=VMEM,
        compiler_params=PARAMS,
        name="collect",
    )(mine[:16], recv.reshape(64 * UNITS, 2, 128)).reshape(8, 16, 2, 2, 128)
    rows = lax.all_to_all(rows, "tp", split_axis=0, concat_axis=0, tiled=True)
    picks = got[:, 16, 1, :64].reshape(64, 2, 32).astype(jnp.int32)
    pos = picks[route, :, mine[16:32]].reshape(32) - 8 * y
    updated = pl.pallas_call(
        update_kernel,
        out_shape=jax.ShapeDtypeStruct(kv_cache.shape, bf),
        in_specs=[SMEM, VMEM, VMEM],
        out_specs=VMEM,
        compiler_params=PARAMS,
        name="update",
    )(pos, kv_cache, rows)

    r2 = jnp.arange(2, dtype=jnp.int32)
    qpos = (jnp.arange(32, dtype=jnp.int32)[:, None] * 64 + picked).reshape(64, 1)
    hit = (picked & 1)[:, None, :] == r2[None, :, None]
    where = jnp.where(hit, (picked // 2)[:, None, :], -1).reshape(64, 2)
    i0 = jnp.broadcast_to(where[:, 0:1], (64, 128))
    i1 = jnp.broadcast_to(where[:, 1:2], (64, 128))
    fr = fresh_kv.reshape(32, 2, 256)
    f0 = jnp.repeat(fr[:, 0], 2, axis=0)
    f1 = jnp.repeat(fr[:, 1], 2, axis=0)
    attn_out = pl.pallas_call(
        attention_kernel,
        out_shape=jax.ShapeDtypeStruct(queries.shape, bf),
        in_specs=[SMEM] + [VMEM] * 9,
        out_specs=VMEM,
        scratch_shapes=ATTEND_SCRATCH,
        compiler_params=PARAMS,
        cost_estimate=pl.CostEstimate(
            flops=4 * 384 * 2048 * 128, bytes_accessed=1500000,
            transcendentals=384 * 2048,
        ),
        name="attend",
    )(
        total[0, :1], recv.reshape(64, 2 * UNITS, 128), queries, f0, f1, i0, i1,
        cos2, sin2, qpos,
    )
    return attn_out, updated


def solution(mesh):
    placed = (P("inst", "tp", None), P("inst"), P("inst", "tp"), P("inst", "tp"), P("inst", None))
    return jax.shard_map(
        local,
        mesh=mesh,
        in_specs=placed,
        out_specs=(P("inst", "tp"), P("inst", "tp", None)),
        check_vma=False,
    )
```

```python
import functools
import math

import jax
import jax.numpy as jnp
from jax import lax
from jax.experimental import pallas as pl
from jax.experimental.pallas import tpu as pltpu
from jax.sharding import PartitionSpec as P

HD = 128
QH = 6
THETA = 1000000.0
CTX = 32
UNITS = 37
VMEM = pl.BlockSpec(memory_space=pltpu.VMEM)
SMEM = pl.BlockSpec(memory_space=pltpu.SMEM)
DISPATCH_SCRATCH = [
    pltpu.VMEM((8, 128), jnp.int32),
    pltpu.SMEM((8, 128), jnp.int32),
    pltpu.SemaphoreType.DMA,
]
ATTEND_SCRATCH = [
    pltpu.VMEM((2048, HD), jnp.bfloat16),
    pltpu.VMEM((2048, HD), jnp.bfloat16),
]
WHOLE = pltpu.CompilerParams(vmem_limit_bytes=66_400_000)
PARAMS = pltpu.CompilerParams(vmem_limit_bytes=40 * 1024 * 1024)


def spread_kernel(own_ref, x_ref, out_ref):
    y = own_ref[1]

    def step(g, carry):
        for k in range(2):
            block = lax.rem(g - y + 8, 8) + 8 * k
            for head in range(8):
                for kv in range(2):
                    lane = head * 256 + kv * 128
                    for pair in range(4):
                        dest = (kv * 32 + g * 4 + pair) * 8 + head
                        out_ref[dest, k] = x_ref[
                            block, pl.ds(2 * pair, 2), pl.ds(lane, 128)
                        ]
        return carry

    lax.fori_loop(0, 8, step, 0)


def dispatch_kernel(
    own_ref, route_ref, r_ref, back_ref, picks_ref, out_ref, slot_ref, packed, tabs, sem
):
    own = own_ref[0]
    route = route_ref[...]
    parts = [route if a == 0 else pltpu.roll(route, 128 - 16 * a, 1) for a in range(8)]
    lane = lax.broadcasted_iota(jnp.int32, (64, 128), 1)
    lanef = lane.astype(jnp.float32)
    ctrl = jnp.concatenate(parts, axis=0).astype(jnp.float32)
    counts = jnp.zeros((64, 128), jnp.float32)
    for l in range(16):
        counts = counts + jnp.where(ctrl[:, l : l + 1] == lanef, 1.0, 0.0)
    row = lax.broadcasted_iota(jnp.int32, (64, 64), 0)
    col = lax.broadcasted_iota(jnp.int32, (64, 64), 1)
    before = (col & 7) * 8 + (col >> 3) < (row & 7) * 8 + (row >> 3)
    starts = jnp.dot(
        jnp.where(before, 1.0, 0.0).astype(jnp.bfloat16), counts.astype(jnp.bfloat16),
        preferred_element_type=jnp.float32,
    ).astype(jnp.int32)
    routes = ctrl.astype(jnp.int32)
    within = jnp.zeros((64, 128), jnp.int32)
    for d in range(1, 16):
        same = (pltpu.roll(ctrl, d, 1) == ctrl) & (lane >= d)
        within = within + jnp.where(same, 1, 0)
    slot = jnp.take_along_axis(starts, routes, axis=1) + within
    first = jnp.sum(jnp.where(lane == own, starts, 0), axis=1, keepdims=True)
    place = routes * UNITS + slot + jnp.where(lane == 0, 4096 * first, 0)
    lane8 = lax.broadcasted_iota(jnp.int32, (8, 128), 1)
    packs = []
    for table in (place, slot):
        acc = table[:8]
        for a in range(1, 8):
            part = pltpu.roll(table[8 * a : 8 * a + 8], 16 * a, 1)
            acc = jnp.where(lane8 // 16 == a, part, acc)
        packs.append(acc)
    packed[...] = packs[0]
    copy = pltpu.make_async_copy(packed, tabs, sem)
    copy.start()
    slot_ref[...] = packs[1]
    copy.wait()
    g = lax.rem(own // 4, 8)

    def step(r, carry):
        for a in range(8):
            h = r * 8 + a
            head = tabs[r, a * 16]
            first = head >> 12
            for y in range(8):
                block = lax.rem(g - y + 8, 8)
                for k in range(2):
                    place = tabs[r, a * 16 + 8 * k + block] & 4095
                    out_ref[place] = r_ref[h * 8 + y, k]
            for s in range(2):
                at = jnp.minimum(first + s, CTX - 1)
                for kv in range(2):
                    out_ref[h * UNITS + CTX + 2 * s + kv] = back_ref[at, kv]
            out_ref[h * UNITS + CTX + 4] = picks_ref[jnp.minimum(first, CTX - 1)]
        return carry

    lax.fori_loop(0, 8, step, 0)


def attention_kernel(
    total_ref, recv_ref, q_ref, f0_ref, f1_ref, i0_ref, i1_ref,
    cos_ref, sin_ref, kpos_ref, qpos_ref, out_ref, keys, vals,
):
    total = total_ref[0]
    cos = cos_ref[...]
    sin = sin_ref[...]
    pick0 = i0_ref[...]
    pick1 = i1_ref[...]
    live = lax.broadcasted_iota(jnp.int32, (64, 128), 0) < 2 * total
    k0 = f0_ref[:, :128].astype(jnp.float32)
    k1 = f1_ref[:, :128].astype(jnp.float32)
    v0 = f0_ref[:, 128:].astype(jnp.float32)
    v1 = f1_ref[:, 128:].astype(jnp.float32)
    for i in range(32):
        at0 = pick0 == i
        at1 = pick1 == i
        k = recv_ref[i, :CTX].reshape(64, HD).astype(jnp.float32)
        k = k * cos + pltpu.roll(k, 64, 1) * sin
        k = jnp.where(at0, k0, jnp.where(at1, k1, k))
        keys[i * 64 : i * 64 + 64, :] = k.astype(jnp.bfloat16)
        v = recv_ref[32 + i, :CTX].reshape(64, HD).astype(jnp.float32)
        v = jnp.where(at0, v0, jnp.where(at1, v1, v))
        v = jnp.where(live, v, 0.0)
        vals[i * 64 : i * 64 + 64, :] = v.astype(jnp.bfloat16)
    allowed = kpos_ref[...] <= qpos_ref[...]
    rowlive = lax.broadcasted_iota(jnp.int32, (64, 128), 0) < 2 * total
    factor = math.log2(math.e) / math.sqrt(HD)
    group = 3
    for base in range(0, QH, group):
        heads = range(base, base + group)
        q = jnp.concatenate([q_ref[:, h * HD : h * HD + HD] for h in heads], axis=0)
        s = lax.dot_general(
            q, keys[...], (((1,), (1,)), ((), ())),
            preferred_element_type=jnp.float32,
        )
        s = jnp.where(allowed[None], s.reshape(group, 64, 2048), -1e30)
        peak = jnp.max(s, axis=2, keepdims=True)
        w = jnp.exp2((s - peak) * factor)
        norm = jnp.sum(w, axis=2, keepdims=True)
        mixed = jnp.dot(
            w.astype(jnp.bfloat16).reshape(group * 64, 2048), vals[...],
            preferred_element_type=jnp.float32,
        ).reshape(group, 64, HD)
        out = jnp.where(rowlive[None], mixed / norm, 0.0)
        for n, h in enumerate(heads):
            out_ref[:, h * HD : h * HD + HD] = out[n].astype(jnp.bfloat16)


def update_kernel(pos_ref, x_ref, rows_ref, out_ref):
    row = lax.broadcasted_iota(jnp.int32, (8, 128), 0)

    def step(l, carry):
        at0 = row == pos_ref[2 * l]
        at1 = row == pos_ref[2 * l + 1]
        for head in range(8):
            for kv in range(2):
                lanes = pl.ds(head * 256 + kv * 128, 128)
                pairf = rows_ref[head, l, kv].astype(jnp.float32)
                old = x_ref[l, :, lanes].astype(jnp.float32)
                new = jnp.where(at0, pairf[0:1], jnp.where(at1, pairf[1:2], old))
                out_ref[l, :, lanes] = new.astype(jnp.bfloat16)
        return carry

    lax.fori_loop(0, 16, step, 0)


def local(kv_cache, route, queries, fresh_kv, picked):
    own = lax.axis_index("inst").astype(jnp.int32)
    y = lax.axis_index("tp").astype(jnp.int32)
    me = jnp.stack([own, y])
    bf = jnp.bfloat16
    spread = pl.pallas_call(
        spread_kernel,
        out_shape=jax.ShapeDtypeStruct((512, 2, 2, 128), bf),
        in_specs=[SMEM, VMEM],
        out_specs=VMEM,
        compiler_params=WHOLE,
        name="spread",
    )(me, kv_cache)
    got = lax.all_to_all(
        spread, ("inst", "tp"), split_axis=0, concat_axis=0, tiled=True
    )
    routes = lax.psum(
        lax.dynamic_update_slice(jnp.zeros((1024,), jnp.int32), route, (own * 16,)),
        "inst",
    )

    half = HD // 2
    freqs = jnp.power(
        jnp.float32(THETA), -2.0 * jnp.arange(half, dtype=jnp.float32) / HD
    )
    shift = (jnp.arange(64, dtype=jnp.int32) // 2 * 64).astype(jnp.float32)
    angle = shift[:, None] * freqs[None, :]
    cos = jnp.cos(angle)
    sin = jnp.sin(angle)
    cos2 = jnp.concatenate([cos, cos], axis=1)
    sin2 = jnp.concatenate([-sin, sin], axis=1)

    fk = fresh_kv[:, :HD].astype(jnp.float32)
    swapped = jnp.concatenate([fk[:, half:], fk[:, :half]], axis=1)
    back_k = (fk * cos2 - swapped * sin2).astype(bf)
    back = jnp.stack(
        [back_k.reshape(32, 2, HD), fresh_kv[:, HD:].reshape(32, 2, HD)], axis=1
    )
    pairs = jnp.stack([picked, jnp.roll(picked, -1, axis=0)], axis=1)
    picks = jnp.pad(pairs.astype(bf), ((0, 0), (0, 0), (0, 126)))

    send, slots = pl.pallas_call(
        dispatch_kernel,
        out_shape=(
            jax.ShapeDtypeStruct((64 * UNITS, 2, 128), bf),
            jax.ShapeDtypeStruct((8, 128), jnp.int32),
        ),
        in_specs=[SMEM, VMEM, VMEM, VMEM, VMEM],
        out_specs=(VMEM, VMEM),
        scratch_shapes=DISPATCH_SCRATCH,
        compiler_params=PARAMS,
        name="dispatch",
    )(own[None], routes.reshape(8, 128), got, back, picks)
    recv = lax.all_to_all(
        send.reshape(64, UNITS, 2, 128), "inst", split_axis=0, concat_axis=0,
        tiled=True,
    )

    local_index = jnp.arange(16, dtype=jnp.int32)
    earlier = (route[:, None] == route[None, :]) & (
        local_index[:, None] > local_index[None, :]
    )
    within = jnp.sum(earlier.astype(jnp.int32), axis=1)
    unit = CTX + 2 * within[:, None] + jnp.arange(2, dtype=jnp.int32)
    rows = recv[
        jnp.broadcast_to(route[None, :, None], (8, 16, 2)),
        jnp.broadcast_to(unit[None], (8, 16, 2)),
    ]
    rows = lax.all_to_all(rows, "tp", split_axis=0, concat_axis=0, tiled=True)
    pos = recv[route, CTX + 4, within, :2].astype(jnp.int32).reshape(32) - 8 * y
    updated = pl.pallas_call(
        update_kernel,
        out_shape=jax.ShapeDtypeStruct(kv_cache.shape, bf),
        in_specs=[SMEM, VMEM, VMEM],
        out_specs=VMEM,
        compiler_params=PARAMS,
        name="update",
    )(pos, kv_cache, rows)

    here = routes == own
    total = jnp.sum(here.astype(jnp.int32))
    j32 = jnp.arange(32, dtype=jnp.int32)
    mine = here[None, :] & (slots.reshape(1, 1024) == j32[:, None])
    index = jnp.arange(1024, dtype=jnp.int32) % 16
    lj = jnp.sum(jnp.where(mine, index[None, :], 0), axis=1)
    g = jnp.arange(8, dtype=jnp.int32)[:, None, None, None]
    pair = jnp.arange(4, dtype=jnp.int32)[None, :, None, None]
    j = j32[None, None, :, None]
    r2 = jnp.arange(2, dtype=jnp.int32)
    kpos = j * 64 + ((g - lj[:, None]) & 7) * 8 + pair * 2 + r2
    kpos = jnp.where(j < total, kpos, 1 << 20).reshape(1, 2048)
    qpos = (j32[:, None] * 64 + picked).reshape(64, 1)
    at = ((picked // 8 + lj[:, None]) & 7) * 4 + (picked & 7) // 2
    hit = (picked & 1)[:, None, :] == r2[None, :, None]
    where = jnp.where(hit, at[:, None, :], -1).reshape(64, 2)
    i0 = jnp.broadcast_to(where[:, 0:1], (64, 128))
    i1 = jnp.broadcast_to(where[:, 1:2], (64, 128))
    fr = fresh_kv.reshape(32, 2, 256)
    f0 = jnp.repeat(fr[:, 0], 2, axis=0)
    f1 = jnp.repeat(fr[:, 1], 2, axis=0)
    attn_out = pl.pallas_call(
        attention_kernel,
        out_shape=jax.ShapeDtypeStruct(queries.shape, bf),
        in_specs=[SMEM] + [VMEM] * 10,
        out_specs=VMEM,
        scratch_shapes=ATTEND_SCRATCH,
        compiler_params=PARAMS,
        cost_estimate=pl.CostEstimate(
            flops=4 * 384 * 2048 * 128, bytes_accessed=1500000,
            transcendentals=384 * 2048,
        ),
        name="attend",
    )(
        total[None], recv, queries, f0, f1, i0, i1, cos2, sin2, kpos, qpos,
    )
    return attn_out, updated


def solution(mesh):
    placed = (P("inst", "tp", None), P("inst"), P("inst", "tp"), P("inst", "tp"), P("inst", None))
    return jax.shard_map(
        local,
        mesh=mesh,
        in_specs=placed,
        out_specs=(P("inst", "tp"), P("inst", "tp", None)),
        check_vma=False,
    )
```

```python
import functools
import math

import jax
import jax.numpy as jnp
from jax import lax
from jax.experimental import pallas as pl
from jax.experimental.pallas import tpu as pltpu
from jax.sharding import PartitionSpec as P

HD = 128
QH = 6
THETA = 1000000.0
CTX = 32
UNITS = 32
STEP = (0, 1, 2, -1)
VMEM = pl.BlockSpec(memory_space=pltpu.VMEM)
SMEM = pl.BlockSpec(memory_space=pltpu.SMEM)
DISPATCH_SCRATCH = [
    pltpu.VMEM((8, 128), jnp.int32),
    pltpu.SMEM((8, 128), jnp.int32),
    pltpu.SemaphoreType.DMA,
]
ATTEND_SCRATCH = [
    pltpu.VMEM((2048, HD), jnp.bfloat16),
    pltpu.VMEM((2048, HD), jnp.bfloat16),
]
WHOLE = pltpu.CompilerParams(vmem_limit_bytes=66_400_000)
PARAMS = pltpu.CompilerParams(vmem_limit_bytes=40 * 1024 * 1024)


def spread_kernel(x_ref, route_ref, picked_ref, out_ref):
    lane = lax.broadcasted_iota(jnp.int32, (2, 128), 1)
    ctrl = jnp.zeros((2, 128), jnp.int32)
    for l in range(16):
        ctrl = jnp.where(lane == l, route_ref[l], ctrl)
        ctrl = ctrl + jnp.where(lane == 64 + route_ref[l], 1, 0)
    picks = jnp.concatenate(
        [picked_ref[0:1, :], picked_ref[1:2, :], jnp.zeros((1, 64), jnp.int32)], axis=1
    )
    row = lax.broadcasted_iota(jnp.int32, (2, 128), 0)
    ctrl = jnp.where(row == 0, ctrl, picks)
    ctrl = ctrl.astype(jnp.float32).astype(jnp.bfloat16)
    for d in range(64):
        out_ref[d, 16] = ctrl

    def step(block, carry):
        for head in range(8):
            for kv in range(2):
                lane = head * 256 + kv * 128
                for pair in range(4):
                    out_ref[head * 8 + kv * 4 + pair, block] = x_ref[
                        block, pl.ds(2 * pair, 2), pl.ds(lane, 128)
                    ]
        return carry

    lax.fori_loop(0, 16, step, 0)


def dispatch_kernel(
    own_ref, r_ref, back_ref, out_ref, ret_ref, tab_ref, total_ref, packed, tabs, sem
):
    own = own_ref[0]
    ctrl = r_ref[:, 16, 0, :].astype(jnp.float32)
    lane = lax.broadcasted_iota(jnp.int32, (64, 128), 1)
    counts = pltpu.roll(ctrl, 64, 1)
    row = lax.broadcasted_iota(jnp.int32, (64, 64), 0)
    col = lax.broadcasted_iota(jnp.int32, (64, 64), 1)
    lower = jnp.where(col < row, 1.0, 0.0).astype(jnp.bfloat16)
    starts = jnp.dot(
        lower, counts.astype(jnp.bfloat16), preferred_element_type=jnp.float32
    ).astype(jnp.int32)
    routes = jnp.where(lane < 16, ctrl, 0.0).astype(jnp.int32)
    within = jnp.zeros((64, 128), jnp.int32)
    for d in range(1, 16):
        same = (pltpu.roll(ctrl, d, 1) == ctrl) & (lane >= d)
        within = within + jnp.where(same, 1, 0)
    slot = jnp.take_along_axis(starts, routes, axis=1) + within
    place = routes * UNITS + slot
    tab_ref[...] = jnp.where(lane < 16, within, pltpu.roll(slot, 16, 1))
    own_z = lax.rem(own, 16)
    own_x = own // 16
    column = jnp.where(lane < 4, lane * 16 + own_z, 0)
    first = jnp.take_along_axis(starts, column, axis=1)
    table = place + 4096 * jnp.where(lane < 4, first, 0)
    lane8 = lax.broadcasted_iota(jnp.int32, (8, 128), 1)
    acc = jnp.zeros((8, 128), jnp.int32)
    for a in range(8):
        part = table[8 * a : 8 * a + 8]
        if a:
            part = pltpu.roll(part, 16 * a, 1)
        acc = jnp.where(lane8 // 16 == a, part, acc)
    packed[...] = acc
    copy = pltpu.make_async_copy(packed, tabs, sem)
    copy.start()
    total = jnp.sum(jnp.where(lane == own, counts, 0.0)).astype(jnp.int32)
    total_ref[...] = jnp.full((1, 128), total, jnp.int32)
    copy.wait()

    def step(a, carry):
        for r in range(8):
            h = a * 8 + r
            place = [tabs[r, a * 16 + l] for l in range(16)]
            units = [r_ref[h, l] for l in range(16)]
            for l in range(16):
                at = place[l] & 4095 if l < 4 else place[l]
                out_ref[at] = units[l]
        return carry

    lax.fori_loop(0, 8, step, 0)
    sign = own_ref[1]

    def returns(u, carry):
        for v in range(4):
            z = lax.rem(own_z + sign * (4 * u + STEP[v]) + 32, 16)
            h = own_x * 16 + z
            for x in range(4):
                away = lax.rem(own_x - x + 4, 4)
                first = tabs[lax.rem(h, 8), h // 8 * 16 + x] >> 12
                for n in range(2):
                    at = jnp.minimum(first + n, CTX - 1)
                    for kv in range(2):
                        out = (v * 4 + u) * 16 + x * 4 + n * 2 + kv
                        ret_ref[out] = back_ref[away, at, kv]
        return carry

    lax.fori_loop(0, 4, returns, 0)


def attention_kernel(
    total_ref, recv_ref, q_ref, f0_ref, f1_ref, i0_ref, i1_ref,
    cos_ref, sin_ref, qpos_ref, out_ref, keys, vals,
):
    total = total_ref[0]
    cos = cos_ref[...]
    sin = sin_ref[...]
    pick0 = i0_ref[...]
    pick1 = i1_ref[...]
    live = lax.broadcasted_iota(jnp.int32, (64, 128), 0) < 2 * total
    k0 = f0_ref[:, :128].astype(jnp.float32)
    k1 = f1_ref[:, :128].astype(jnp.float32)
    v0 = f0_ref[:, 128:].astype(jnp.float32)
    v1 = f1_ref[:, 128:].astype(jnp.float32)
    for i in range(32):
        at0 = pick0 == i
        at1 = pick1 == i
        src = i // 4 * 8 + i % 4
        k = recv_ref[src, : 2 * CTX, :].astype(jnp.float32)
        k = k * cos + pltpu.roll(k, 64, 1) * sin
        k = jnp.where(at0, k0, jnp.where(at1, k1, k))
        keys[i * 64 : i * 64 + 64, :] = k.astype(jnp.bfloat16)
        v = recv_ref[src + 4, : 2 * CTX, :].astype(jnp.float32)
        v = jnp.where(at0, v0, jnp.where(at1, v1, v))
        v = jnp.where(live, v, 0.0)
        vals[i * 64 : i * 64 + 64, :] = v.astype(jnp.bfloat16)
    col = lax.broadcasted_iota(jnp.int32, (64, 2048), 1)
    kpos = (col & 63) // 2 * 64 + (col >> 6) * 2 + (col & 1)
    allowed = (kpos <= qpos_ref[...]) & (kpos < total * 64)
    rowlive = lax.broadcasted_iota(jnp.int32, (64, 128), 0) < 2 * total
    factor = math.log2(math.e) / math.sqrt(HD)
    group = 3
    for base in range(0, QH, group):
        heads = range(base, base + group)
        q = jnp.concatenate([q_ref[:, h * HD : h * HD + HD] for h in heads], axis=0)
        s = lax.dot_general(
            q, keys[...], (((1,), (1,)), ((), ())),
            preferred_element_type=jnp.float32,
        )
        s = jnp.where(allowed[None], s.reshape(group, 64, 2048), -1e30)
        peak = jnp.max(s, axis=2, keepdims=True)
        w = jnp.exp2((s - peak) * factor)
        norm = jnp.sum(w, axis=2, keepdims=True)
        mixed = jnp.dot(
            w.astype(jnp.bfloat16).reshape(group * 64, 2048), vals[...],
            preferred_element_type=jnp.float32,
        ).reshape(group, 64, HD)
        out = jnp.where(rowlive[None], mixed / norm, 0.0)
        for n, h in enumerate(heads):
            out_ref[:, h * HD : h * HD + HD] = out[n].astype(jnp.bfloat16)


def update_kernel(pos_ref, x_ref, rows_ref, out_ref):
    row = lax.broadcasted_iota(jnp.int32, (8, 128), 0)

    def step(l, carry):
        at0 = row == pos_ref[2 * l]
        at1 = row == pos_ref[2 * l + 1]
        for head in range(8):
            for kv in range(2):
                lanes = pl.ds(head * 256 + kv * 128, 128)
                pairf = rows_ref[head, l, kv].astype(jnp.float32)
                old = x_ref[l, :, lanes].astype(jnp.float32)
                new = jnp.where(at0, pairf[0:1], jnp.where(at1, pairf[1:2], old))
                out_ref[l, :, lanes] = new.astype(jnp.bfloat16)
        return carry

    lax.fori_loop(0, 16, step, 0)


def local(kv_cache, route, queries, fresh_kv, picked):
    own = lax.axis_index("inst").astype(jnp.int32)
    y = lax.axis_index("tp").astype(jnp.int32)
    bf = jnp.bfloat16
    spread = pl.pallas_call(
        spread_kernel,
        out_shape=jax.ShapeDtypeStruct((64, 17, 2, 128), bf),
        in_specs=[VMEM, SMEM, VMEM],
        out_specs=VMEM,
        compiler_params=WHOLE,
        name="spread",
    )(kv_cache, route, picked.T)
    halfway = lax.all_to_all(spread, "tp", split_axis=0, concat_axis=0, tiled=True)

    half = HD // 2
    freqs = jnp.power(
        jnp.float32(THETA), -2.0 * jnp.arange(half, dtype=jnp.float32) / HD
    )
    shift = (jnp.arange(64, dtype=jnp.int32) // 2 * 64).astype(jnp.float32)
    angle = shift[:, None] * freqs[None, :]
    cos = jnp.cos(angle)
    sin = jnp.sin(angle)
    cos2 = jnp.concatenate([cos, cos], axis=1)
    sin2 = jnp.concatenate([-sin, sin], axis=1)

    fk = fresh_kv[:, :HD].astype(jnp.float32)
    swapped = jnp.concatenate([fk[:, half:], fk[:, :half]], axis=1)
    back_k = (fk * cos2 - swapped * sin2).astype(bf)
    back = jnp.stack(
        [back_k.reshape(32, 2, HD), fresh_kv[:, HD:].reshape(32, 2, HD)], axis=1
    )

    heads = tuple(range(8))
    mesh_axes = ("inst", "tp")

    def shifted(values, x_step, z_step):
        pairs = []
        for x in range(4):
            for z in range(16):
                for t in heads:
                    to = (x + x_step) % 4 * 16 + (z + z_step * (1 - 2 * (t % 2))) % 16
                    pairs.append(((x * 16 + z) * 8 + t, to * 8 + t))
        return lax.ppermute(values, mesh_axes, pairs)

    back, halfway = lax.optimization_barrier((back, halfway))
    got = lax.all_to_all(halfway, "inst", split_axis=0, concat_axis=0, tiled=True)
    backs = jnp.stack([back] + [shifted(back, n, 0) for n in (1, 2, 3)])

    sign = 1 - 2 * (y % 2)
    send, ret, tab, total = pl.pallas_call(
        dispatch_kernel,
        out_shape=(
            jax.ShapeDtypeStruct((64 * UNITS, 2, 128), bf),
            jax.ShapeDtypeStruct((256, 2, 128), bf),
            jax.ShapeDtypeStruct((64, 128), jnp.int32),
            jax.ShapeDtypeStruct((1, 128), jnp.int32),
        ),
        in_specs=[SMEM, VMEM, VMEM],
        out_specs=(VMEM, VMEM, VMEM, VMEM),
        scratch_shapes=DISPATCH_SCRATCH,
        compiler_params=PARAMS,
        name="dispatch",
    )(jnp.stack([own, sign]), got, backs)
    recv = lax.all_to_all(
        send.reshape(64, UNITS, 2, 128), "inst", split_axis=0, concat_axis=0,
        tiled=True,
    )

    ret = ret.reshape(4, 4, 16, 2, 128)
    ret = [ret[0]] + [shifted(ret[v], 0, STEP[v]) for v in (1, 2, 3)]
    ret = [jnp.stack([part[u] for part in ret]) for u in range(4)]
    ret = jnp.stack([ret[0]] + [shifted(ret[u], 0, 4 * u) for u in (1, 2, 3)])
    mine = lax.dynamic_index_in_dim(tab, own, 0, keepdims=False)
    dz = (sign * (own % 16 - route % 16)) & 15
    v = dz & 3
    u = ((dz + 1) // 4) & 3
    at = (u * 4 + v) * 8 + route // 16 * 2 + mine[:16]
    rows = ret.reshape(128, 2, 2, 128)[at]
    rows = lax.all_gather(rows, "tp", axis=0, tiled=False)
    picks = got[:, 16, 1, :64].reshape(64, 2, 32).astype(jnp.int32)
    pos = picks[route, :, mine[16:32]].reshape(32) - 8 * y
    updated = pl.pallas_call(
        update_kernel,
        out_shape=jax.ShapeDtypeStruct(kv_cache.shape, bf),
        in_specs=[SMEM, VMEM, VMEM],
        out_specs=VMEM,
        compiler_params=PARAMS,
        name="update",
    )(pos, kv_cache, rows)

    r2 = jnp.arange(2, dtype=jnp.int32)
    qpos = (jnp.arange(32, dtype=jnp.int32)[:, None] * 64 + picked).reshape(64, 1)
    hit = (picked & 1)[:, None, :] == r2[None, :, None]
    where = jnp.where(hit, (picked // 2)[:, None, :], -1).reshape(64, 2)
    i0 = jnp.broadcast_to(where[:, 0:1], (64, 128))
    i1 = jnp.broadcast_to(where[:, 1:2], (64, 128))
    fr = fresh_kv.reshape(32, 2, 256)
    f0 = jnp.repeat(fr[:, 0], 2, axis=0)
    f1 = jnp.repeat(fr[:, 1], 2, axis=0)
    attn_out = pl.pallas_call(
        attention_kernel,
        out_shape=jax.ShapeDtypeStruct(queries.shape, bf),
        in_specs=[SMEM] + [VMEM] * 9,
        out_specs=VMEM,
        scratch_shapes=ATTEND_SCRATCH,
        compiler_params=PARAMS,
        cost_estimate=pl.CostEstimate(
            flops=4 * 384 * 2048 * 128, bytes_accessed=1500000,
            transcendentals=384 * 2048,
        ),
        name="attend",
    )(
        total[0, :1], recv.reshape(64, 2 * UNITS, 128), queries, f0, f1, i0, i1,
        cos2, sin2, qpos,
    )
    return attn_out, updated


def solution(mesh):
    placed = (P("inst", "tp", None), P("inst"), P("inst", "tp"), P("inst", "tp"), P("inst", None))
    return jax.shard_map(
        local,
        mesh=mesh,
        in_specs=placed,
        out_specs=(P("inst", "tp"), P("inst", "tp", None)),
        check_vma=False,
    )
```

```python
import functools
import math

import jax
import jax.numpy as jnp
from jax import lax
from jax.experimental import pallas as pl
from jax.experimental.pallas import tpu as pltpu
from jax.sharding import PartitionSpec as P

HD = 128
QH = 6
THETA = 1000000.0
CTX = 32
UNITS = 36
VMEM = pl.BlockSpec(memory_space=pltpu.VMEM)
SMEM = pl.BlockSpec(memory_space=pltpu.SMEM)
DISPATCH_SCRATCH = [
    pltpu.VMEM((8, 128), jnp.int32),
    pltpu.SMEM((8, 128), jnp.int32),
    pltpu.SemaphoreType.DMA,
]
ATTEND_SCRATCH = [
    pltpu.VMEM((2048, HD), jnp.bfloat16),
    pltpu.VMEM((2048, HD), jnp.bfloat16),
]
WHOLE = pltpu.CompilerParams(vmem_limit_bytes=66_400_000)
PARAMS = pltpu.CompilerParams(vmem_limit_bytes=40 * 1024 * 1024)


def spread_kernel(x_ref, route_ref, picked_ref, out_ref):
    lane = lax.broadcasted_iota(jnp.int32, (2, 128), 1)
    ctrl = jnp.zeros((2, 128), jnp.int32)
    for l in range(16):
        ctrl = jnp.where(lane == l, route_ref[l], ctrl)
        ctrl = ctrl + jnp.where(lane == 64 + route_ref[l], 1, 0)
    picks = jnp.concatenate(
        [picked_ref[0:1, :], picked_ref[1:2, :], jnp.zeros((1, 64), jnp.int32)], axis=1
    )
    row = lax.broadcasted_iota(jnp.int32, (2, 128), 0)
    ctrl = jnp.where(row == 0, ctrl, picks)
    ctrl = ctrl.astype(jnp.float32).astype(jnp.bfloat16)
    for d in range(64):
        out_ref[d, 16] = ctrl

    def step(block, carry):
        for head in range(8):
            for kv in range(2):
                lane = head * 256 + kv * 128
                for pair in range(4):
                    out_ref[head * 8 + kv * 4 + pair, block] = x_ref[
                        block, pl.ds(2 * pair, 2), pl.ds(lane, 128)
                    ]
        return carry

    lax.fori_loop(0, 16, step, 0)


def dispatch_kernel(own_ref, r_ref, back_ref, out_ref, tab_ref, total_ref, packed, tabs, sem):
    own = own_ref[0]
    ctrl = r_ref[:, 16, 0, :].astype(jnp.float32)
    lane = lax.broadcasted_iota(jnp.int32, (64, 128), 1)
    counts = pltpu.roll(ctrl, 64, 1)
    row = lax.broadcasted_iota(jnp.int32, (64, 64), 0)
    col = lax.broadcasted_iota(jnp.int32, (64, 64), 1)
    lower = jnp.where(col < row, 1.0, 0.0).astype(jnp.bfloat16)
    starts = jnp.dot(
        lower, counts.astype(jnp.bfloat16), preferred_element_type=jnp.float32
    ).astype(jnp.int32)
    routes = jnp.where(lane < 16, ctrl, 0.0).astype(jnp.int32)
    within = jnp.zeros((64, 128), jnp.int32)
    for d in range(1, 16):
        same = (pltpu.roll(ctrl, d, 1) == ctrl) & (lane >= d)
        within = within + jnp.where(same, 1, 0)
    slot = jnp.take_along_axis(starts, routes, axis=1) + within
    place = routes * UNITS + slot
    ret = routes * UNITS + CTX + 2 * within
    tab_ref[...] = jnp.where(lane < 16, ret, pltpu.roll(slot, 16, 1))
    own_lane = lane == own
    first = jnp.sum(jnp.where(own_lane, starts, 0), axis=1, keepdims=True)
    table = place + jnp.where(lane == 0, 4096 * first, 0)
    lane8 = lax.broadcasted_iota(jnp.int32, (8, 128), 1)
    acc = jnp.zeros((8, 128), jnp.int32)
    for a in range(8):
        part = table[8 * a : 8 * a + 8]
        if a:
            part = pltpu.roll(part, 16 * a, 1)
        acc = jnp.where(lane8 // 16 == a, part, acc)
    packed[...] = acc
    copy = pltpu.make_async_copy(packed, tabs, sem)
    copy.start()
    total = jnp.sum(jnp.where(own_lane, counts, 0.0)).astype(jnp.int32)
    total_ref[...] = jnp.full((1, 128), total, jnp.int32)
    copy.wait()

    def step(a, carry):
        for r in range(8):
            h = a * 8 + r
            place = [tabs[r, a * 16 + l] for l in range(16)]
            first = place[0] >> 12
            place[0] = place[0] & 4095
            units = [r_ref[h, l] for l in range(16)]
            slots = [jnp.minimum(first + s, CTX - 1) for s in range(2)]
            backs = [back_ref[slots[s], kv] for s in range(2) for kv in range(2)]
            for l in range(16):
                out_ref[place[l]] = units[l]
            for n in range(4):
                out_ref[h * UNITS + CTX + n] = backs[n]
        return carry

    lax.fori_loop(0, 8, step, 0)


def attention_kernel(
    total_ref, recv_ref, q_ref, f0_ref, f1_ref, i0_ref, i1_ref,
    cos_ref, sin_ref, qpos_ref, out_ref, keys, vals,
):
    total = total_ref[0]
    cos = cos_ref[...]
    sin = sin_ref[...]
    pick0 = i0_ref[...]
    pick1 = i1_ref[...]
    live = lax.broadcasted_iota(jnp.int32, (64, 128), 0) < 2 * total
    k0 = f0_ref[:, :128].astype(jnp.float32)
    k1 = f1_ref[:, :128].astype(jnp.float32)
    v0 = f0_ref[:, 128:].astype(jnp.float32)
    v1 = f1_ref[:, 128:].astype(jnp.float32)
    for i in range(32):
        at0 = pick0 == i
        at1 = pick1 == i
        src = i // 4 * 8 + i % 4
        k = recv_ref[src, : 2 * CTX, :].astype(jnp.float32)
        k = k * cos + pltpu.roll(k, 64, 1) * sin
        k = jnp.where(at0, k0, jnp.where(at1, k1, k))
        keys[i * 64 : i * 64 + 64, :] = k.astype(jnp.bfloat16)
        v = recv_ref[src + 4, : 2 * CTX, :].astype(jnp.float32)
        v = jnp.where(at0, v0, jnp.where(at1, v1, v))
        v = jnp.where(live, v, 0.0)
        vals[i * 64 : i * 64 + 64, :] = v.astype(jnp.bfloat16)
    col = lax.broadcasted_iota(jnp.int32, (64, 2048), 1)
    kpos = (col & 63) // 2 * 64 + (col >> 6) * 2 + (col & 1)
    allowed = (kpos <= qpos_ref[...]) & (kpos < total * 64)
    rowlive = lax.broadcasted_iota(jnp.int32, (64, 128), 0) < 2 * total
    factor = math.log2(math.e) / math.sqrt(HD)
    group = 3
    for base in range(0, QH, group):
        heads = range(base, base + group)
        q = jnp.concatenate([q_ref[:, h * HD : h * HD + HD] for h in heads], axis=0)
        s = lax.dot_general(
            q, keys[...], (((1,), (1,)), ((), ())),
            preferred_element_type=jnp.float32,
        )
        s = jnp.where(allowed[None], s.reshape(group, 64, 2048), -1e30)
        peak = jnp.max(s, axis=2, keepdims=True)
        w = jnp.exp2((s - peak) * factor)
        norm = jnp.sum(w, axis=2, keepdims=True)
        mixed = jnp.dot(
            w.astype(jnp.bfloat16).reshape(group * 64, 2048), vals[...],
            preferred_element_type=jnp.float32,
        ).reshape(group, 64, HD)
        out = jnp.where(rowlive[None], mixed / norm, 0.0)
        for n, h in enumerate(heads):
            out_ref[:, h * HD : h * HD + HD] = out[n].astype(jnp.bfloat16)


def update_kernel(pos_ref, x_ref, rows_ref, out_ref, done, sems):
    row = lax.broadcasted_iota(jnp.int32, (8, 128), 0)
    copies = []
    for l in range(16):
        at0 = row == pos_ref[2 * l]
        at1 = row == pos_ref[2 * l + 1]
        for head in range(8):
            for kv in range(2):
                lanes = pl.ds(head * 256 + kv * 128, 128)
                pair = rows_ref[head, l, kv].astype(jnp.float32)
                old = x_ref[l, :, lanes].astype(jnp.float32)
                new = jnp.where(at0, pair[0:1], jnp.where(at1, pair[1:2], old))
                done[l, :, lanes] = new.astype(jnp.bfloat16)
        if l % 4 == 3:
            part = pl.ds(l - 3, 4)
            copy = pltpu.make_async_copy(
                done.at[part], out_ref.at[part], sems.at[l // 4]
            )
            copy.start()
            copies.append(copy)
    for copy in copies:
        copy.wait()


def local(kv_cache, route, queries, fresh_kv, picked):
    own = lax.axis_index("inst").astype(jnp.int32)
    y = lax.axis_index("tp").astype(jnp.int32)
    bf = jnp.bfloat16
    spread = pl.pallas_call(
        spread_kernel,
        out_shape=jax.ShapeDtypeStruct((64, 17, 2, 128), bf),
        in_specs=[VMEM, SMEM, VMEM],
        out_specs=VMEM,
        compiler_params=WHOLE,
        name="spread",
    )(kv_cache, route, picked.T)
    got = lax.all_to_all(spread, "tp", split_axis=0, concat_axis=0, tiled=True)
    got = lax.all_to_all(got, "inst", split_axis=0, concat_axis=0, tiled=True)

    half = HD // 2
    freqs = jnp.power(
        jnp.float32(THETA), -2.0 * jnp.arange(half, dtype=jnp.float32) / HD
    )
    shift = (jnp.arange(64, dtype=jnp.int32) // 2 * 64).astype(jnp.float32)
    angle = shift[:, None] * freqs[None, :]
    cos = jnp.cos(angle)
    sin = jnp.sin(angle)
    cos2 = jnp.concatenate([cos, cos], axis=1)
    sin2 = jnp.concatenate([-sin, sin], axis=1)

    fk = fresh_kv[:, :HD].astype(jnp.float32)
    swapped = jnp.concatenate([fk[:, half:], fk[:, :half]], axis=1)
    back_k = (fk * cos2 - swapped * sin2).astype(bf)
    back = jnp.stack(
        [back_k.reshape(32, 2, HD), fresh_kv[:, HD:].reshape(32, 2, HD)], axis=1
    )

    send, tab, total = pl.pallas_call(
        dispatch_kernel,
        out_shape=(
            jax.ShapeDtypeStruct((64 * UNITS, 2, 128), bf),
            jax.ShapeDtypeStruct((64, 128), jnp.int32),
            jax.ShapeDtypeStruct((1, 128), jnp.int32),
        ),
        in_specs=[SMEM, VMEM, VMEM],
        out_specs=(VMEM, VMEM, VMEM),
        scratch_shapes=DISPATCH_SCRATCH,
        compiler_params=PARAMS,
        name="dispatch",
    )(own[None], got, back)
    recv = lax.all_to_all(
        send.reshape(64, UNITS, 2, 128), "inst", split_axis=0, concat_axis=0,
        tiled=True,
    )

    mine = lax.dynamic_index_in_dim(tab, own, 0, keepdims=False)
    units = recv.reshape(64, UNITS // 2, 2, 2, 128)
    at = mine[:16] - route * UNITS
    rows = units[
        jnp.broadcast_to(route, (8, 16)), jnp.broadcast_to(at // 2, (8, 16))
    ]
    rows = lax.all_to_all(rows, "tp", split_axis=0, concat_axis=0, tiled=True)
    picks = got[:, 16, 1, :64].reshape(64, 2, 32).astype(jnp.int32)
    pos = picks[route, :, mine[16:32]].reshape(32) - 8 * y
    updated = pl.pallas_call(
        update_kernel,
        out_shape=jax.ShapeDtypeStruct(kv_cache.shape, bf),
        in_specs=[SMEM, VMEM, VMEM],
        out_specs=pl.BlockSpec(memory_space=pl.ANY),
        scratch_shapes=[
            pltpu.VMEM(kv_cache.shape, bf), pltpu.SemaphoreType.DMA((4,)),
        ],
        compiler_params=PARAMS,
        name="update",
    )(pos, kv_cache, rows)

    r2 = jnp.arange(2, dtype=jnp.int32)
    qpos = (jnp.arange(32, dtype=jnp.int32)[:, None] * 64 + picked).reshape(64, 1)
    hit = (picked & 1)[:, None, :] == r2[None, :, None]
    where = jnp.where(hit, (picked // 2)[:, None, :], -1).reshape(64, 2)
    i0 = jnp.broadcast_to(where[:, 0:1], (64, 128))
    i1 = jnp.broadcast_to(where[:, 1:2], (64, 128))
    fr = fresh_kv.reshape(32, 2, 256)
    f0 = jnp.repeat(fr[:, 0], 2, axis=0)
    f1 = jnp.repeat(fr[:, 1], 2, axis=0)
    attn_out = pl.pallas_call(
        attention_kernel,
        out_shape=jax.ShapeDtypeStruct(queries.shape, bf),
        in_specs=[SMEM] + [VMEM] * 9,
        out_specs=VMEM,
        scratch_shapes=ATTEND_SCRATCH,
        compiler_params=PARAMS,
        cost_estimate=pl.CostEstimate(
            flops=4 * 384 * 2048 * 128, bytes_accessed=1500000,
            transcendentals=384 * 2048,
        ),
        name="attend",
    )(
        total[0, :1], recv.reshape(64, 2 * UNITS, 128), queries, f0, f1, i0, i1,
        cos2, sin2, qpos,
    )
    return attn_out, updated


def solution(mesh):
    placed = (P("inst", "tp", None), P("inst"), P("inst", "tp"), P("inst", "tp"), P("inst", None))
    return jax.shard_map(
        local,
        mesh=mesh,
        in_specs=placed,
        out_specs=(P("inst", "tp"), P("inst", "tp", None)),
        check_vma=False,
    )
```

```python
import functools
import math

import jax
import jax.numpy as jnp
from jax import lax
from jax.experimental import pallas as pl
from jax.experimental.pallas import tpu as pltpu
from jax.sharding import PartitionSpec as P

HD = 128
QH = 6
THETA = 1000000.0
CTX = 32
UNITS = 36
VMEM = pl.BlockSpec(memory_space=pltpu.VMEM)
SMEM = pl.BlockSpec(memory_space=pltpu.SMEM)
DISPATCH_SCRATCH = [
    pltpu.VMEM((8, 128), jnp.int32),
    pltpu.SMEM((8, 128), jnp.int32),
    pltpu.SemaphoreType.DMA,
]
ATTEND_SCRATCH = [
    pltpu.VMEM((2048, HD), jnp.bfloat16),
    pltpu.VMEM((2048, HD), jnp.bfloat16),
]
WHOLE = pltpu.CompilerParams(vmem_limit_bytes=66_400_000)
PARAMS = pltpu.CompilerParams(vmem_limit_bytes=40 * 1024 * 1024)


def spread_kernel(x_ref, route_ref, picked_ref, out_ref):
    lane = lax.broadcasted_iota(jnp.int32, (2, 128), 1)
    ctrl = jnp.zeros((2, 128), jnp.int32)
    for l in range(16):
        ctrl = jnp.where(lane == l, route_ref[l], ctrl)
        ctrl = ctrl + jnp.where(lane == 64 + route_ref[l], 1, 0)
    picks = jnp.concatenate(
        [picked_ref[0:1, :], picked_ref[1:2, :], jnp.zeros((1, 64), jnp.int32)], axis=1
    )
    row = lax.broadcasted_iota(jnp.int32, (2, 128), 0)
    ctrl = jnp.where(row == 0, ctrl, picks)
    ctrl = ctrl.astype(jnp.float32).astype(jnp.bfloat16)
    for d in range(64):
        out_ref[d, 16] = ctrl

    def step(block, carry):
        for head in range(8):
            for kv in range(2):
                lane = head * 256 + kv * 128
                for pair in range(4):
                    out_ref[head * 8 + kv * 4 + pair, block] = x_ref[
                        block, pl.ds(2 * pair, 2), pl.ds(lane, 128)
                    ]
        return carry

    lax.fori_loop(0, 16, step, 0)


def dispatch_kernel(own_ref, r_ref, back_ref, out_ref, tab_ref, total_ref, packed, tabs, sem):
    own = own_ref[0]
    ctrl = r_ref[:, 16, 0, :].astype(jnp.float32)
    lane = lax.broadcasted_iota(jnp.int32, (64, 128), 1)
    counts = pltpu.roll(ctrl, 64, 1)
    row = lax.broadcasted_iota(jnp.int32, (64, 64), 0)
    col = lax.broadcasted_iota(jnp.int32, (64, 64), 1)
    lower = jnp.where(col < row, 1.0, 0.0).astype(jnp.bfloat16)
    starts = jnp.dot(
        lower, counts.astype(jnp.bfloat16), preferred_element_type=jnp.float32
    ).astype(jnp.int32)
    routes = jnp.where(lane < 16, ctrl, 0.0).astype(jnp.int32)
    within = jnp.zeros((64, 128), jnp.int32)
    for d in range(1, 16):
        same = (pltpu.roll(ctrl, d, 1) == ctrl) & (lane >= d)
        within = within + jnp.where(same, 1, 0)
    slot = jnp.take_along_axis(starts, routes, axis=1) + within
    place = routes * UNITS + slot
    ret = routes * UNITS + CTX + 2 * within
    tab_ref[...] = jnp.where(lane < 16, ret, pltpu.roll(slot, 16, 1))
    own_lane = lane == own
    first = jnp.sum(jnp.where(own_lane, starts, 0), axis=1, keepdims=True)
    table = place + jnp.where(lane == 0, 4096 * first, 0)
    lane8 = lax.broadcasted_iota(jnp.int32, (8, 128), 1)
    acc = jnp.zeros((8, 128), jnp.int32)
    for a in range(8):
        part = table[8 * a : 8 * a + 8]
        if a:
            part = pltpu.roll(part, 16 * a, 1)
        acc = jnp.where(lane8 // 16 == a, part, acc)
    packed[...] = acc
    copy = pltpu.make_async_copy(packed, tabs, sem)
    copy.start()
    total = jnp.sum(jnp.where(own_lane, counts, 0.0)).astype(jnp.int32)
    total_ref[...] = jnp.full((1, 128), total, jnp.int32)
    copy.wait()

    def step(a, carry):
        for r in range(8):
            h = a * 8 + r
            place = [tabs[r, a * 16 + l] for l in range(16)]
            first = place[0] >> 12
            place[0] = place[0] & 4095
            units = [r_ref[h, l] for l in range(16)]
            slots = [jnp.minimum(first + s, CTX - 1) for s in range(2)]
            backs = [back_ref[slots[s], kv] for s in range(2) for kv in range(2)]
            for l in range(16):
                out_ref[place[l]] = units[l]
            for n in range(4):
                out_ref[h * UNITS + CTX + n] = backs[n]
        return carry

    lax.fori_loop(0, 8, step, 0)


def collect_kernel(info_ref, recv_ref, out_ref):
    for l in range(16):
        for kv in range(2):
            unit = recv_ref[info_ref[l] + kv]
            for t in range(8):
                out_ref[t * 32 + l * 2 + kv] = unit


def attention_kernel(
    total_ref, recv_ref, q_ref, f0_ref, f1_ref, i0_ref, i1_ref,
    cos_ref, sin_ref, qpos_ref, out_ref, keys, vals,
):
    total = total_ref[0]
    cos = cos_ref[...]
    sin = sin_ref[...]
    pick0 = i0_ref[...]
    pick1 = i1_ref[...]
    live = lax.broadcasted_iota(jnp.int32, (64, 128), 0) < 2 * total
    k0 = f0_ref[:, :128].astype(jnp.float32)
    k1 = f1_ref[:, :128].astype(jnp.float32)
    v0 = f0_ref[:, 128:].astype(jnp.float32)
    v1 = f1_ref[:, 128:].astype(jnp.float32)
    for i in range(32):
        at0 = pick0 == i
        at1 = pick1 == i
        src = i // 4 * 8 + i % 4
        k = recv_ref[src, : 2 * CTX, :].astype(jnp.float32)
        k = k * cos + pltpu.roll(k, 64, 1) * sin
        k = jnp.where(at0, k0, jnp.where(at1, k1, k))
        keys[i * 64 : i * 64 + 64, :] = k.astype(jnp.bfloat16)
        v = recv_ref[src + 4, : 2 * CTX, :].astype(jnp.float32)
        v = jnp.where(at0, v0, jnp.where(at1, v1, v))
        v = jnp.where(live, v, 0.0)
        vals[i * 64 : i * 64 + 64, :] = v.astype(jnp.bfloat16)
    col = lax.broadcasted_iota(jnp.int32, (64, 2048), 1)
    kpos = (col & 63) // 2 * 64 + (col >> 6) * 2 + (col & 1)
    allowed = (kpos <= qpos_ref[...]) & (kpos < total * 64)
    rowlive = lax.broadcasted_iota(jnp.int32, (64, 128), 0) < 2 * total
    factor = math.log2(math.e) / math.sqrt(HD)
    group = 3
    for base in range(0, QH, group):
        heads = range(base, base + group)
        q = jnp.concatenate([q_ref[:, h * HD : h * HD + HD] for h in heads], axis=0)
        s = lax.dot_general(
            q, keys[...], (((1,), (1,)), ((), ())),
            preferred_element_type=jnp.float32,
        )
        s = jnp.where(allowed[None], s.reshape(group, 64, 2048), -1e30)
        peak = jnp.max(s, axis=2, keepdims=True)
        w = jnp.exp2((s - peak) * factor)
        norm = jnp.sum(w, axis=2, keepdims=True)
        mixed = jnp.dot(
            w.astype(jnp.bfloat16).reshape(group * 64, 2048), vals[...],
            preferred_element_type=jnp.float32,
        ).reshape(group, 64, HD)
        out = jnp.where(rowlive[None], mixed / norm, 0.0)
        for n, h in enumerate(heads):
            out_ref[:, h * HD : h * HD + HD] = out[n].astype(jnp.bfloat16)


def update_kernel(pos_ref, x_ref, rows_ref, out_ref, done, sems):
    row = lax.broadcasted_iota(jnp.int32, (8, 128), 0)
    copies = []
    for l in range(16):
        at0 = row == pos_ref[2 * l]
        at1 = row == pos_ref[2 * l + 1]
        for head in range(8):
            for kv in range(2):
                lanes = pl.ds(head * 256 + kv * 128, 128)
                pair = rows_ref[head, l, kv].astype(jnp.float32)
                old = x_ref[l, :, lanes].astype(jnp.float32)
                new = jnp.where(at0, pair[0:1], jnp.where(at1, pair[1:2], old))
                done[l, :, lanes] = new.astype(jnp.bfloat16)
        if l % 4 == 3:
            part = pl.ds(l - 3, 4)
            copy = pltpu.make_async_copy(
                done.at[part], out_ref.at[part], sems.at[l // 4]
            )
            copy.start()
            copies.append(copy)
    for copy in copies:
        copy.wait()


def local(kv_cache, route, queries, fresh_kv, picked):
    own = lax.axis_index("inst").astype(jnp.int32)
    y = lax.axis_index("tp").astype(jnp.int32)
    bf = jnp.bfloat16
    spread = pl.pallas_call(
        spread_kernel,
        out_shape=jax.ShapeDtypeStruct((64, 17, 2, 128), bf),
        in_specs=[VMEM, SMEM, VMEM],
        out_specs=VMEM,
        compiler_params=WHOLE,
        name="spread",
    )(kv_cache, route, picked.T)
    got = lax.all_to_all(spread, "tp", split_axis=0, concat_axis=0, tiled=True)
    got = lax.all_to_all(got, "inst", split_axis=0, concat_axis=0, tiled=True)

    half = HD // 2
    freqs = jnp.power(
        jnp.float32(THETA), -2.0 * jnp.arange(half, dtype=jnp.float32) / HD
    )
    shift = (jnp.arange(64, dtype=jnp.int32) // 2 * 64).astype(jnp.float32)
    angle = shift[:, None] * freqs[None, :]
    cos = jnp.cos(angle)
    sin = jnp.sin(angle)
    cos2 = jnp.concatenate([cos, cos], axis=1)
    sin2 = jnp.concatenate([-sin, sin], axis=1)

    fk = fresh_kv[:, :HD].astype(jnp.float32)
    swapped = jnp.concatenate([fk[:, half:], fk[:, :half]], axis=1)
    back_k = (fk * cos2 - swapped * sin2).astype(bf)
    back = jnp.stack(
        [back_k.reshape(32, 2, HD), fresh_kv[:, HD:].reshape(32, 2, HD)], axis=1
    )

    send, tab, total = pl.pallas_call(
        dispatch_kernel,
        out_shape=(
            jax.ShapeDtypeStruct((64 * UNITS, 2, 128), bf),
            jax.ShapeDtypeStruct((64, 128), jnp.int32),
            jax.ShapeDtypeStruct((1, 128), jnp.int32),
        ),
        in_specs=[SMEM, VMEM, VMEM],
        out_specs=(VMEM, VMEM, VMEM),
        scratch_shapes=DISPATCH_SCRATCH,
        compiler_params=PARAMS,
        name="dispatch",
    )(own[None], got, back)
    recv = lax.all_to_all(
        send.reshape(64, UNITS, 2, 128), "inst", split_axis=0, concat_axis=0,
        tiled=True,
    )

    mine = lax.dynamic_index_in_dim(tab, own, 0, keepdims=False)
    rows = pl.pallas_call(
        collect_kernel,
        out_shape=jax.ShapeDtypeStruct((256, 2, 128), bf),
        in_specs=[SMEM, VMEM],
        out_specs=VMEM,
        compiler_params=PARAMS,
        name="collect",
    )(mine[:16], recv.reshape(64 * UNITS, 2, 128)).reshape(8, 16, 2, 2, 128)
    rows = lax.all_to_all(rows, "tp", split_axis=0, concat_axis=0, tiled=True)
    picks = got[:, 16, 1, :64].reshape(64, 2, 32).astype(jnp.int32)
    pos = picks[route, :, mine[16:32]].reshape(32) - 8 * y
    updated = pl.pallas_call(
        update_kernel,
        out_shape=jax.ShapeDtypeStruct(kv_cache.shape, bf),
        in_specs=[SMEM, VMEM, VMEM],
        out_specs=pl.BlockSpec(memory_space=pl.ANY),
        scratch_shapes=[
            pltpu.VMEM(kv_cache.shape, bf), pltpu.SemaphoreType.DMA((4,)),
        ],
        compiler_params=PARAMS,
        name="update",
    )(pos, kv_cache, rows)

    r2 = jnp.arange(2, dtype=jnp.int32)
    qpos = (jnp.arange(32, dtype=jnp.int32)[:, None] * 64 + picked).reshape(64, 1)
    hit = (picked & 1)[:, None, :] == r2[None, :, None]
    where = jnp.where(hit, (picked // 2)[:, None, :], -1).reshape(64, 2)
    i0 = jnp.broadcast_to(where[:, 0:1], (64, 128))
    i1 = jnp.broadcast_to(where[:, 1:2], (64, 128))
    fr = fresh_kv.reshape(32, 2, 256)
    f0 = jnp.repeat(fr[:, 0], 2, axis=0)
    f1 = jnp.repeat(fr[:, 1], 2, axis=0)
    attn_out = pl.pallas_call(
        attention_kernel,
        out_shape=jax.ShapeDtypeStruct(queries.shape, bf),
        in_specs=[SMEM] + [VMEM] * 9,
        out_specs=VMEM,
        scratch_shapes=ATTEND_SCRATCH,
        compiler_params=PARAMS,
        cost_estimate=pl.CostEstimate(
            flops=4 * 384 * 2048 * 128, bytes_accessed=1500000,
            transcendentals=384 * 2048,
        ),
        name="attend",
    )(
        total[0, :1], recv.reshape(64, 2 * UNITS, 128), queries, f0, f1, i0, i1,
        cos2, sin2, qpos,
    )
    return attn_out, updated


def solution(mesh):
    placed = (P("inst", "tp", None), P("inst"), P("inst", "tp"), P("inst", "tp"), P("inst", None))
    return jax.shard_map(
        local,
        mesh=mesh,
        in_specs=placed,
        out_specs=(P("inst", "tp"), P("inst", "tp", None)),
        check_vma=False,
    )
```
